256 devices in a mesh: section: 2 (over core), dp: 32 (over z, x), mp: 4 (over y).
Axes of the slice: x: 4, y: 4, z: 8, core: 2. Of those that a mesh axis runs over, the one named last changes fastest.
Arguments:
- prompt_state: bfloat16 [1024, 2048], P(('section', 'dp')), may hold values from -6 to 6
- beam_parent: int32 [1024, 4, 16], P(('section', 'dp')), may hold values from 0 to 15
- beam_code: int32 [1024, 4, 16], P(('section', 'dp')), may hold values from 0 to 255
- norm_gain: float32 [2048], replicated, may hold values from 0.1 to 1.9
- up_weight: bfloat16 [2048, 4096], P(None, 'mp'), may hold values from -0.125 to 0.125
- down_weight: bfloat16 [4096, 2048], P('mp'), may hold values from -0.09375 to 0.09375
- code_table: bfloat16 [256, 2048], replicated, may hold values from -6 to 6
- item_features: bfloat16 [32768, 1024], P('dp'), may hold values from -6 to 6
- lookup_owner: int32 [1024, 384, 1], P(('section', 'dp', 'mp')), may hold values from 0 to 31; in each aligned block of 1536 rows (0 to 1535, 1536 to 3071, ..., all dimensions but the last counted through in order) at most 96 rows name the same one
- lookup_row: int32 [1024, 384], P(('section', 'dp', 'mp')), may hold values from 0 to 1023
- cand_count: int32 [1024], P(('section', 'dp', 'mp')), may hold values from 16 to 128
- item_proj: bfloat16 [1024, 384], replicated, may hold values from -0.1875 to 0.1875
- user_proj: bfloat16 [2048, 256], replicated, may hold values from -0.125 to 0.125
- rank_bias: float32 [256], replicated, may hold values from -3 to 3
- out_weight: float32 [256], replicated, may hold values from -0.375 to 0.375
Outputs:
- logits: float32 [1024, 128], P(('section', 'dp', 'mp'))
- user_state: bfloat16 [1024, 2048], P(('section', 'dp'))
The draws below stay inside these ranges and needn't reach their ends.
Inputs may be any that keep to these rules, and one draw needn't show every extreme that they name: `lookup_owner`: among the lookups of one device (1536 aligned rows) no owner is named more than 96 times, a bound that some block reaches.
All inputs are finite; a program needn't handle non-finite values.
Results may differ from the reference program's by a relative error of at most 0.035.
Values may be sent and summed in bfloat16 or wider, within the bound.
No kernel may reach another device: no remote copies, remote signals or barrier semaphores. Data moves between devices by JAX's collectives and lax.ppermute only.
A program may use at most 128 MiB of HBM per device.

```python
import math
import jax
import jax.numpy as jnp
import numpy as np
from jax import lax

D = 2048
FF = 4096
CODES = 256
BEAM = 16
STEPS = 4
REQ_DEV = 16
FEAT = 1024
ATT = 128
VALW = 256
CMAX = 128
HIST = 256
P_SIZE = 1024
RQ = 4
SLOTS = 384
CAP = 96
ITEMS_DEV = 1024
ITEMS = 32768
N_DP = 32
N_MP = 4


def set_ends(drawn, key, least, high):
    dims = drawn.shape
    place = [jax.random.randint(jax.random.fold_in(key, axis), (), 0, dims[axis]) for axis in range(len(dims))]
    drawn = drawn.at[tuple(place)].set(least)
    longest = dims.index(max(dims))
    place[longest] = (place[longest] + 1) % dims[longest]
    return drawn.at[tuple(place)].set(high)


def block_scale(rng, extent, pieces, least, high):
    def one(axis_at, parts):
        heights = jax.random.uniform(jax.random.fold_in(jax.random.fold_in(rng, 6), axis_at), (parts,), jnp.float32, least / len(pieces), high / len(pieces))
        return jnp.repeat(jnp.exp(heights), extent[axis_at] // parts).reshape((-1,) + (1,) * (len(extent) - axis_at - 1))

    gain = one(*pieces[0])
    for cut in pieces[1:]:
        gain = gain * one(*cut)
    return gain


def deal_out(own_key, own, number, rows, amount, top, bound, lean):
    sequence = jax.random.permutation(own_key, amount)
    crowded, ordinary = portions_of(amount, rows * top, bound, lean, True), portions_of(amount, rows * top, bound, lean, False)
    places = jnp.arange(amount)

    def named(tallies, turn):
        used = int((tallies > 0).sum())
        fixed = max(1, used // 4)
        moved = fixed + (places - fixed + turn * (used - fixed)) % max(1, amount - fixed)
        return jnp.zeros((amount,), jnp.int32).at[sequence[jnp.where(places < fixed, places, moved)]].set(jnp.asarray(tallies, jnp.int32))

    tallies = jnp.where(number % 4 == 0, named(crowded, number // 4), named(ordinary, number - number // 4 - 1))
    mixed = jax.random.permutation(jax.random.fold_in(own, 3), amount)
    giver, receiver = mixed[0:amount // 2 * 2:2], mixed[1:amount // 2 * 2:2]
    margin = jnp.minimum(tallies[giver] - 1, bound - tallies[receiver]) // 2
    margin = jnp.where((giver == sequence[0]) | (receiver == sequence[0]) | (tallies[receiver] == 0), 0, jnp.maximum(margin, 0))
    moved = jax.random.randint(jax.random.fold_in(own, 4), (amount // 2,), 0, 1 << 20) % (margin + 1)
    tallies = tallies.at[giver].add(-moved).at[receiver].add(moved)
    items = jnp.searchsorted(jnp.cumsum(tallies), jnp.arange(rows * top), side="right").astype(jnp.int32)
    table = items.reshape(top, rows).T
    table = table[jax.random.permutation(jax.random.fold_in(own, 1), rows)]
    turn = jax.random.randint(jax.random.fold_in(own, 2), (rows, 1), 0, top)
    return jnp.take_along_axis(table, (jnp.arange(top)[None, :] + turn) % top, axis=1)


def portions_of(count, total, most, skew, full):
    loads = [(1 << 20) // math.isqrt(grade ** skew) + 1 for grade in range(1, count + 1)]
    largest = most if full else min(most, max(-(-total // count), total * loads[0] // sum(loads)))
    least = 1 if total - largest >= count - 1 else 0
    given, rest = [largest] + [least] * (count - 1), total - largest - least * (count - 1)
    while rest > 0:
        free = [i for i in range(1, count) if given[i] < largest] or [i for i in range(1, count) if given[i] < most]
        whole, budget = sum([loads[i] for i in free]), rest
        for i in free:
            more = min(most - given[i], max(1, budget * loads[i] // whole), rest)
            given[i] = given[i] + more
            rest = rest - more
    return np.array(given)


def centred(stream_key, extent, scale, limit, cuts=(), kind=jnp.bfloat16):
    gain = block_scale(stream_key, extent, cuts, -0.22, 0.18) if cuts else 1.0
    drawn = jax.random.normal(stream_key, extent, jnp.float32) * scale * gain
    return jnp.minimum(jnp.maximum(drawn, -limit), limit).astype(kind)


def setup_inputs(seed: int = 0) -> dict:
    streams_of = jax.random.split(jax.random.key(seed), 16)
    prompt_state = centred(streams_of[0], (P_SIZE, D), 1.0, 6.0, ((0, 64),))
    beam_parent = set_ends(jax.random.randint(streams_of[1], (P_SIZE, STEPS, BEAM), 0, BEAM), jax.random.fold_in(streams_of[1], 1), 0, BEAM - 1).astype(jnp.int32)
    beam_code = set_ends(jax.random.randint(streams_of[2], (P_SIZE, STEPS, BEAM), 0, CODES), jax.random.fold_in(streams_of[2], 1), 0, CODES - 1).astype(jnp.int32)
    norm_gain = jnp.clip(1.0 + 0.18 * jax.random.normal(streams_of[3], (D,), jnp.float32), 0.1, 1.9)
    up_weight = centred(streams_of[4], (D, FF), D ** -0.5, 0.125, ((1, 4),))
    down_weight = centred(streams_of[5], (FF, D), FF ** -0.5, 0.09375, ((0, 4),))
    code_table = centred(streams_of[6], (CODES, D), 1.0, 6.0)
    item_features = centred(streams_of[7], (ITEMS, FEAT), 1.0, 6.0, ((0, 32),))
    lookup_owner_keys = jax.random.split(jax.random.fold_in(streams_of[8], 1), P_SIZE * SLOTS // (RQ * SLOTS))
    lookup_owner_turns = jax.random.permutation(jax.random.fold_in(streams_of[8], 3), P_SIZE * SLOTS // (RQ * SLOTS))
    lookup_owner = jax.vmap(lambda own, number: deal_out(jax.random.fold_in(streams_of[8], 2), own, number, RQ * SLOTS, N_DP, 1, CAP, 2))(lookup_owner_keys, lookup_owner_turns).reshape((P_SIZE, SLOTS, 1))
    lookup_row = set_ends(jax.random.randint(streams_of[9], (P_SIZE, SLOTS), 0, ITEMS_DEV), jax.random.fold_in(streams_of[9], 1), 0, ITEMS_DEV - 1).astype(jnp.int32)
    cand_count = set_ends(jax.random.randint(streams_of[10], (P_SIZE,), max(1, CMAX // 8), CMAX + 1), jax.random.fold_in(streams_of[10], 1), max(1, CMAX // 8), CMAX).astype(jnp.int32)
    item_proj = centred(streams_of[11], (FEAT, ATT + VALW), FEAT ** -0.5, 0.1875)
    user_proj = centred(streams_of[12], (D, VALW), D ** -0.5, 0.125)
    rank_bias = centred(streams_of[13], (VALW,), 0.5, 3.0, (), jnp.float32)
    out_weight = centred(streams_of[14], (VALW,), VALW ** -0.5, 0.375, (), jnp.float32)
    return dict(prompt_state=prompt_state, beam_parent=beam_parent, beam_code=beam_code, norm_gain=norm_gain, up_weight=up_weight, down_weight=down_weight, code_table=code_table, item_features=item_features, lookup_owner=lookup_owner, lookup_row=lookup_row, cand_count=cand_count, item_proj=item_proj, user_proj=user_proj, rank_bias=rank_bias, out_weight=out_weight)


def normalize(values, gain_row):
    squares = lax.optimization_barrier(jnp.mean(values * values, axis=-1, keepdims=True))
    return values * lax.rsqrt(squares + 1e-06) * gain_row

def retrieve(inputs, norm_gain, up_weight, down_weight, code_table):
    prompt_rows, parents, code_ids = inputs
    hidden_cut = FF // N_MP
    beam_state = jnp.broadcast_to(prompt_rows[:, None, :], (REQ_DEV, BEAM, D)).reshape(REQ_DEV * BEAM, D)
    for beam_step in range(STEPS):
        wide_state = beam_state.astype(jnp.float32)
        normed = normalize(wide_state, norm_gain).astype(jnp.bfloat16)
        raised = jnp.dot(normed, up_weight, preferred_element_type=jnp.float32)
        active = jax.nn.gelu(raised).astype(jnp.bfloat16)
        summed = jnp.zeros((REQ_DEV * BEAM, D), jnp.float32)
        for piece_index in range(N_MP):
            lower = piece_index * hidden_cut
            partial_sum = jnp.dot(active[:, lower:lower + hidden_cut], down_weight[lower:lower + hidden_cut], preferred_element_type=jnp.float32)
            rounded = lax.optimization_barrier(partial_sum.astype(jnp.bfloat16))
            summed = summed + rounded.astype(jnp.float32)
        middle = (wide_state + summed).astype(jnp.bfloat16).reshape(REQ_DEV, BEAM, D)
        moved_rows = jnp.take_along_axis(middle, parents[:, beam_step, :, None], axis=1)
        code_rows = code_table[code_ids[:, beam_step, :]]
        beam_state = (moved_rows.astype(jnp.float32) + code_rows.astype(jnp.float32)).astype(jnp.bfloat16).reshape(REQ_DEV * BEAM, D)
    pooled = lax.optimization_barrier(jnp.mean(beam_state.astype(jnp.float32).reshape(REQ_DEV, BEAM, D), axis=1))
    return pooled.astype(jnp.bfloat16)

def score(projected, counts, user_rows, user_proj, rank_bias, out_weight):
    queries = projected[:, :CMAX, :ATT].astype(jnp.float32)
    key_part = projected[:, CMAX:, :ATT].astype(jnp.float32)
    cand_part = projected[:, :CMAX, ATT:].astype(jnp.float32)
    hist_part = projected[:, CMAX:, ATT:].astype(jnp.float32)
    scores = jnp.einsum('bcd,bhd->bch', queries, key_part) / math.sqrt(ATT)
    weights = jax.nn.sigmoid(scores).astype(jnp.bfloat16).astype(jnp.float32)
    interest = jnp.einsum('bch,bhv->bcv', weights, hist_part) / math.sqrt(HIST)
    user_term = jnp.dot(user_rows, user_proj, preferred_element_type=jnp.float32)
    hidden = jax.nn.relu(interest + cand_part + user_term[:, None, :] + rank_bias)
    outcome = jnp.einsum('bcv,v->bc', hidden, out_weight, precision=lax.Precision.HIGHEST)
    live_slot = jnp.arange(CMAX)[None, :] < counts[:, None]
    return jnp.where(live_slot, outcome, jnp.float32(0.0))

def rank(inputs, item_features, item_proj, user_proj, rank_bias, out_weight):
    item_ids, counts, user_rows = inputs
    item_rows = item_features[item_ids]
    projected = jnp.dot(item_rows.reshape(-1, FEAT), item_proj, preferred_element_type=jnp.float32)
    projected = projected.astype(jnp.bfloat16).reshape(RQ, SLOTS, ATT + VALW)
    return score(projected, counts, user_rows, user_proj, rank_bias, out_weight)

def reference(prompt_state, beam_parent, beam_code, norm_gain, up_weight, down_weight, code_table, item_features, lookup_owner, lookup_row, cand_count, item_proj, user_proj, rank_bias, out_weight):
    groups = prompt_state.shape[0] // REQ_DEV
    user_rows = lax.map(lambda inputs: retrieve(inputs, norm_gain, up_weight, down_weight, code_table), (prompt_state.reshape(groups, REQ_DEV, D), beam_parent.reshape(groups, REQ_DEV, STEPS, BEAM), beam_code.reshape(groups, REQ_DEV, STEPS, BEAM))).reshape(-1, D)
    rolled = jnp.roll(user_rows, user_rows.shape[0] // 2, axis=0)
    item_ids = (lookup_owner[:, :, 0] * ITEMS_DEV + lookup_row).astype(jnp.int32)
    blocks = item_ids.shape[0] // RQ
    logits = lax.map(lambda inputs: rank(inputs, item_features, item_proj, user_proj, rank_bias, out_weight), (item_ids.reshape(blocks, RQ, SLOTS), cand_count.reshape(blocks, RQ), rolled.reshape(blocks, RQ, D))).reshape(-1, CMAX)
    return (logits, user_rows)
```

```python
import functools
import math

import jax
import jax.numpy as jnp
from jax import lax
from jax.experimental import pallas as pl
from jax.experimental.pallas import tpu as pltpu
from jax.sharding import PartitionSpec as P

ATT = 128
CMAX = 128
HIST = 256
UP_CUTS = 4
DOWN_CUTS = 4
BF = jnp.bfloat16
F32 = jnp.float32
NT = (((1,), (1,)), ((), ()))

VMEM = pl.BlockSpec(memory_space=pltpu.VMEM)
SMEM = pl.BlockSpec(memory_space=pltpu.SMEM)
ANY = pl.BlockSpec(memory_space=pl.ANY)


def dot(a, b):
    return jnp.dot(a, b, preferred_element_type=F32)


def call(kernel, name, out_shape, in_specs, out_specs, scratch=(), limit=32, flops=0, moved=0):
    return pl.pallas_call(
        kernel,
        name=name,
        out_shape=out_shape,
        in_specs=in_specs,
        out_specs=out_specs,
        scratch_shapes=list(scratch),
        compiler_params=pltpu.CompilerParams(vmem_limit_bytes=limit * 2**20),
        cost_estimate=pl.CostEstimate(flops=flops, bytes_accessed=moved, transcendentals=0),
    )


def shift(value, axis, by):
    size = lax.axis_size(axis)
    return lax.ppermute(value, axis, [(i, (i + by) % size) for i in range(size)])


def swapped(value, axis, bit):
    mask = 2**bit
    pairs = [(source, source ^ mask) for source in range(lax.axis_size(axis))]
    return lax.ppermute(value, axis, pairs)


def normalize(values, gain_row):
    squares = jnp.mean(values * values, axis=-1, keepdims=True)
    return values * lax.rsqrt(squares + 1e-06) * gain_row


def weight_copies(up_ref, down_ref, up_s, down_s, sems):
    wide = up_s.shape[2]
    tall = down_s.shape[2]
    ups = [
        pltpu.make_async_copy(up_ref.at[:, pl.ds(c * wide, wide)], up_s.at[c], sems.at[c])
        for c in range(UP_CUTS)
    ]
    downs = [
        pltpu.make_async_copy(
            down_ref.at[:, pl.ds(c * tall, tall)], down_s.at[c], sems.at[UP_CUTS + c]
        )
        for c in range(DOWN_CUTS)
    ]
    return ups, downs


def raise_rows(normed, ups, up_s, act_s):
    wide = up_s.shape[2]
    for c in range(UP_CUTS):
        ups[c].wait()
        act_s[:, c * wide : (c + 1) * wide] = jax.nn.gelu(dot(normed, up_s[c])).astype(BF)


def weight_scratch(rows, width, hidden):
    return (
        pltpu.VMEM((UP_CUTS, width, hidden // UP_CUTS), BF),
        pltpu.VMEM((DOWN_CUTS, hidden, width // DOWN_CUTS), BF),
        pltpu.VMEM((rows, hidden), BF),
        pltpu.SemaphoreType.DMA((UP_CUTS + DOWN_CUTS,)),
    )


def first_kernel(prompt, gain, up, down, out, up_s, down_s, act_s, sems):
    ups, downs = weight_copies(up, down, up_s, down_s, sems)
    for copy in ups + downs:
        copy.start()
    normed = normalize(prompt[...].astype(F32), gain[...]).astype(BF)
    raise_rows(normed, ups, up_s, act_s)
    tall = down_s.shape[2]
    for c in range(DOWN_CUTS):
        downs[c].wait()
        out[:, c * tall : (c + 1) * tall] = dot(act_s[...], down_s[c]).astype(BF)


def second_kernel(
    place, prompt, t0, t1, t2, t3, code_rows, gain, up, down,
    o0, o1, o2, o3, state, up_s, down_s, act_s, sems, middle_s, normed_s,
):
    ups, downs = weight_copies(up, down, up_s, down_s, sems)
    for copy in ups + downs:
        copy.start()
    requests = prompt.shape[0]
    beams = code_rows.shape[0] // requests
    own = o0.shape[0]
    total = (
        t0[...].astype(F32) + t1[...].astype(F32) + t2[...].astype(F32) + t3[...].astype(F32)
    )
    middle = (prompt[...].astype(F32) + total).astype(BF).astype(F32)
    middle_s[0:requests, :] = middle
    middle_s[requests : 2 * requests, :] = middle
    base = place[0]
    for r in range(requests):
        row = middle_s[pl.ds(base + r, 1), :]
        now = (row + code_rows[r * beams : (r + 1) * beams, :].astype(F32)).astype(BF)
        if (r + 1) * beams <= own:
            state[r * beams : (r + 1) * beams, :] = now
        normed_s[r * beams : (r + 1) * beams, :] = normalize(now.astype(F32), gain[...]).astype(BF)
    raise_rows(normed_s[...], ups, up_s, act_s)
    lower(act_s, downs, down_s, (o0, o1, o2, o3))


def lower(act_s, downs, down_s, outs):
    tall = down_s.shape[2]
    own = outs[0].shape[0]
    for c in range(DOWN_CUTS):
        downs[c].wait()
        part = dot(act_s[...], down_s[c]).astype(BF)
        for k, out in enumerate(outs):
            out[:, c * tall : (c + 1) * tall] = part[k * own : (k + 1) * own, :]


def third_kernel(
    n0, n1, n2, n3, up, down, o0, o1, o2, o3, up_s, down_s, act_s, sems, normed_s
):
    ups, downs = weight_copies(up, down, up_s, down_s, sems)
    for copy in ups + downs:
        copy.start()
    own = n0.shape[0]
    for k, ref in enumerate((n0, n1, n2, n3)):
        normed_s[k * own : (k + 1) * own, :] = ref[...]
    raise_rows(normed_s[...], ups, up_s, act_s)
    lower(act_s, downs, down_s, (o0, o1, o2, o3))


def last_kernel(
    n0, n1, n2, n3, pool, base, up, down, out, up_s, down_s, act_s, sems, normed_s
):
    ups, downs = weight_copies(up, down, up_s, down_s, sems)
    for copy in ups + downs:
        copy.start()
    own = n0.shape[0]
    for k, ref in enumerate((n0, n1, n2, n3)):
        normed_s[k * own : (k + 1) * own, :] = ref[...]
    raise_rows(normed_s[...], ups, up_s, act_s)
    mixed = dot(pool[...], act_s[...]).astype(BF)
    tall = down_s.shape[2]
    for c in range(DOWN_CUTS):
        downs[c].wait()
        cut = slice(c * tall, (c + 1) * tall)
        out[:, cut] = (dot(mixed, down_s[c]) + base[:, cut]).astype(BF)


def advance(t0, t1, t2, t3, state, parent, code_rows):
    rows = state.shape[0]
    total = (
        t0[...].astype(F32) + t1[...].astype(F32) + t2[...].astype(F32) + t3[...].astype(F32)
    )
    middle = (state[...].astype(F32) + total).astype(BF)
    chosen = (parent[...] == lax.broadcasted_iota(jnp.int32, (rows, rows), 1)).astype(BF)
    return (dot(chosen, middle) + code_rows[...].astype(F32)).astype(BF)


def owner_kernel(t0, t1, t2, t3, state, parent, code_rows, gain, out_state, out_normed):
    now = advance(t0, t1, t2, t3, state, parent, code_rows)
    out_state[...] = now
    out_normed[...] = normalize(now.astype(F32), gain[...]).astype(BF)


def owner_last_kernel(
    t0, t1, t2, t3, state, parent, code_rows, gain, pool, mean_code, out_base, out_normed
):
    now = advance(t0, t1, t2, t3, state, parent, code_rows)
    out_normed[...] = normalize(now.astype(F32), gain[...]).astype(BF)
    rows = state.shape[0]
    out_base[...] = dot(pool[:, :rows], now) + mean_code[...]


def prepare_kernel(
    place, code0, code12, code3, parent3, table, rows0, rows1, rows2, mean_code, pool
):
    codes = table.shape[0]
    requests, beams = parent3.shape
    spots = requests * beams

    def picked(column):
        ids = lax.broadcasted_iota(jnp.int32, (column.shape[0], codes), 1)
        return dot((column == ids).astype(BF), table[...]).astype(BF)

    rows0[...] = picked(code0[...])
    half = rows1.shape[0]
    both = picked(code12[...])
    rows1[...] = both[:half, :]
    rows2[...] = both[half:, :]
    tally = jnp.zeros((requests, codes), F32)
    ids = lax.broadcasted_iota(jnp.int32, (requests, codes), 1)
    kids = jnp.zeros((requests, spots), F32)
    lanes = lax.broadcasted_iota(jnp.int32, (requests, spots), 1)
    for b in range(beams):
        tally = tally + (code3[:, b : b + 1] == ids).astype(F32)
        kids = kids + (parent3[:, b : b + 1] == lanes % beams).astype(F32)
    mean_code[...] = dot((tally / beams).astype(BF), table[...])
    held = (place[0] + lanes // beams) % requests
    mine = held == lax.broadcasted_iota(jnp.int32, (requests, spots), 0)
    pool[...] = jnp.where(mine, kids / beams, 0.0).astype(BF)


def pool_kernel(t0, t1, t2, t3, out):
    out[...] = (
        t0[...].astype(F32) + t1[...].astype(F32) + t2[...].astype(F32) + t3[...].astype(F32)
    ).astype(BF)


def index_kernel(owners, local_rows, outgoing, target):
    requests, slots = owners.shape
    count, capacity = outgoing.shape
    before = (
        lax.broadcasted_iota(jnp.int32, (slots, slots), 0)
        < lax.broadcasted_iota(jnp.int32, (slots, slots), 1)
    ).astype(BF)
    names = lax.broadcasted_iota(jnp.int32, (count, slots), 0)
    places = lax.broadcasted_iota(jnp.int32, (128, slots), 0)
    carry = jnp.zeros((count, 1), F32)
    low = jnp.zeros((count, 128), F32)
    high = jnp.zeros((count, 128), F32)
    for q in range(requests):
        owner = owners[q : q + 1, :]
        row = local_rows[q : q + 1, :]
        named = (owner == names).astype(F32)
        ahead = dot(named.astype(BF), before) + carry
        carry = carry + jnp.sum(named, axis=1, keepdims=True)
        position = jnp.sum(named * ahead, axis=0, keepdims=True).astype(jnp.int32)
        target[q : q + 1, :] = owner * capacity + position
        spot = (places == position).astype(BF)
        low = low + lax.dot_general(
            (named * (row & 31).astype(F32)).astype(BF), spot, NT, preferred_element_type=F32
        )
        high = high + lax.dot_general(
            (named * (row >> 5).astype(F32)).astype(BF), spot, NT, preferred_element_type=F32
        )
    outgoing[...] = (high * 32.0 + low).astype(jnp.int32)[:, :capacity]


def serve_kernel(wanted, table, out, *, group):
    rows = table.shape[0]
    asking = wanted.shape[1]
    capacity = wanted.shape[0]
    ids = lax.broadcasted_iota(jnp.int32, (capacity * group, rows), 1)
    for g in range(asking // group):
        column = jnp.concatenate(
            [wanted[:, g * group + k : g * group + k + 1] for k in range(group)], axis=0
        )
        found = dot((column == ids).astype(BF), table[...]).astype(BF)
        for k in range(group):
            out[g * group + k] = found[k * capacity : (k + 1) * capacity, :]


def rank_kernel(target, returned, bias, out):
    requests = out.shape[0]
    count, capacity, width = returned.shape
    table = returned[...].reshape(count * capacity, width)
    slots = target.shape[0]
    ids = lax.broadcasted_iota(jnp.int32, (slots, count * capacity), 1)
    for q in range(requests):
        rows = dot((target[:, q : q + 1] == ids).astype(BF), table).astype(BF)
        queries = rows[:CMAX, :ATT]
        keys = rows[CMAX:, :ATT]
        scores = lax.dot_general(queries, keys, NT, preferred_element_type=F32) / math.sqrt(ATT)
        weights = jax.nn.sigmoid(scores).astype(BF)
        interest = dot(weights, rows[CMAX:, ATT:]) / math.sqrt(HIST)
        out[q] = interest + rows[:CMAX, ATT:].astype(F32) + bias[...]


def logit_kernel(place, counts, users, user_proj, units, weight, out, term_s):
    term_s[...] = dot(users[...], user_proj[...])
    requests = units.shape[0]
    lanes = lax.broadcasted_iota(jnp.int32, (1, CMAX), 1)
    for q in range(requests):
        hidden = jnp.maximum(units[q] + term_s[pl.ds(place[0] + q, 1), :], 0.0)
        line = lax.dot_general(
            weight[...], hidden, NT, preferred_element_type=F32, precision=lax.Precision.HIGHEST
        )
        out[q : q + 1, :] = jnp.where(lanes < counts[q], line, 0.0)


def body(
    prompt_state,
    beam_parent,
    beam_code,
    norm_gain,
    up_weight,
    down_weight,
    code_table,
    item_features,
    lookup_owner,
    lookup_row,
    cand_count,
    item_proj,
    user_proj,
    rank_bias,
    out_weight,
):
    requests, width = prompt_state.shape
    beams = beam_parent.shape[2]
    hidden = up_weight.shape[1]
    rows = requests * beams
    rank_rows, slots = lookup_row.shape
    own = rank_rows * beams
    owner_count = lax.axis_size("dp")
    capacity = max(2, 2 * rank_rows * slots // owner_count)
    first = lax.axis_index("mp") * rank_rows
    place = first.astype(jnp.int32).reshape(1)
    gain = norm_gain.reshape(1, width)
    shape = jax.ShapeDtypeStruct

    outgoing, target = call(
        index_kernel, "index",
        (shape((owner_count, capacity), jnp.int32), shape((rank_rows, slots), jnp.int32)),
        [VMEM, VMEM], (VMEM, VMEM), limit=16, flops=200_000_000, moved=100_000,
    )(lookup_owner.reshape(rank_rows, slots), lookup_row)
    wanted = lax.all_to_all(outgoing, "dp", split_axis=0, concat_axis=0, tiled=True)

    ffn = dict(limit=32, flops=4 * rows * width * hidden, moved=4 * width * hidden)
    weights_spec = [ANY, ANY]
    part = call(
        first_kernel, "ffn0", shape((requests, width), BF),
        [VMEM, VMEM] + weights_spec, VMEM, weight_scratch(requests, width, hidden),
        limit=32, flops=rows * width * hidden, moved=4 * width * hidden,
    )(prompt_state, gain, up_weight, down_weight)
    parts = [shift(part, "mp", k) for k in (1, 2, 3)]

    table = jnp.dot(item_features, item_proj, preferred_element_type=F32).astype(BF)

    def turned(value):
        twice = jnp.concatenate([value, value], axis=0)
        return lax.dynamic_slice_in_dim(twice, first, requests, 0)

    codes = turned(beam_code)
    parents = turned(beam_parent)
    block = jnp.arange(own, dtype=jnp.int32)[:, None] // beams * beams
    code0 = codes[:, 0, :].reshape(rows, 1)
    code12 = jnp.concatenate(
        [codes[:rank_rows, 1, :].reshape(own, 1), codes[:rank_rows, 2, :].reshape(own, 1)]
    )
    parent1 = parents[:rank_rows, 1, :].reshape(own, 1) + block
    parent2 = parents[:rank_rows, 2, :].reshape(own, 1) + block
    request_ids = jnp.arange(requests)[:, None]
    mine = (request_ids >= first) & (request_ids < first + rank_rows)
    code3 = jnp.where(mine, beam_code[:, 3, :], -1)
    parent3 = beam_parent[:, 3, :]
    rows0, rows1, rows2, mean_code, pool = call(
        prepare_kernel, "prepare",
        (
            shape((rows, width), BF), shape((own, width), BF), shape((own, width), BF),
            shape((requests, width), F32), shape((requests, rows), BF),
        ),
        [SMEM] + [VMEM] * 5, (VMEM,) * 5, limit=24,
        flops=2 * 400 * 256 * width, moved=3_000_000,
    )(place, code0, code12, code3, parent3, code_table)

    quarter = (shape((own, width), BF),) * 4
    *outs, state = call(
        second_kernel, "ffn1", quarter + (shape((own, width), BF),),
        [SMEM] + [VMEM] * 7 + weights_spec, (VMEM,) * 5,
        weight_scratch(rows, width, hidden)
        + (pltpu.VMEM((2 * requests, width), F32), pltpu.VMEM((rows, width), BF)),
        **ffn,
    )(place, prompt_state, part, *parts, rows0, gain, up_weight, down_weight)
    sums = [outs[0]] + [shift(outs[k], "mp", k) for k in (1, 2, 3)]
    state, normed = call(
        owner_kernel, "owner1", (shape((own, width), BF),) * 2, [VMEM] * 8, (VMEM,) * 2,
        limit=16, flops=2 * own * own * width, moved=2_000_000,
    )(*sums, state, parent1, rows1, gain)

    others = [normed] + [shift(normed, "mp", -k) for k in (1, 2, 3)]
    outs = call(
        third_kernel, "ffn2", quarter, [VMEM] * 4 + weights_spec, (VMEM,) * 4,
        weight_scratch(rows, width, hidden) + (pltpu.VMEM((rows, width), BF),),
        **ffn,
    )(*others, up_weight, down_weight)
    sums = [outs[0]] + [shift(outs[k], "mp", k) for k in (1, 2, 3)]
    base, normed = call(
        owner_last_kernel, "owner2", (shape((requests, width), F32), shape((own, width), BF)),
        [VMEM] * 10, (VMEM,) * 2,
        limit=16, flops=2 * own * own * width, moved=2_000_000,
    )(*sums, state, parent2, rows2, gain, pool, mean_code)

    others = [normed] + [shift(normed, "mp", -k) for k in (1, 2, 3)]
    part = call(
        last_kernel, "ffn3", shape((requests, width), BF), [VMEM] * 6 + weights_spec, VMEM,
        weight_scratch(rows, width, hidden) + (pltpu.VMEM((rows, width), BF),),
        **ffn,
    )(*others, pool, base, up_weight, down_weight)
    parts = [shift(part, "mp", k) for k in (1, 2, 3)]
    pooled = call(
        pool_kernel, "pool", shape((requests, width), BF), [VMEM] * 4, VMEM,
        limit=16, flops=100_000, moved=400_000,
    )(part, *parts)
    partner = swapped(pooled, "section", 0)

    served = call(
        functools.partial(serve_kernel, group=4), "serve",
        shape((owner_count, capacity, table.shape[1]), BF), [VMEM] * 2, VMEM,
        limit=32, flops=2 * owner_count * capacity * table.shape[0] * table.shape[1],
        moved=4_000_000,
    )(wanted.T, table)
    returned = lax.all_to_all(served, "dp", split_axis=0, concat_axis=0, tiled=True)
    units = call(
        rank_kernel, "rank", shape((rank_rows, CMAX, table.shape[1] - ATT), F32),
        [VMEM] * 3, VMEM, limit=48,
        flops=2 * rank_rows * slots * owner_count * capacity * table.shape[1], moved=4_000_000,
    )(target.T, returned, rank_bias.reshape(1, -1))
    logits = call(
        logit_kernel, "logit", shape((rank_rows, CMAX), F32), [SMEM, SMEM] + [VMEM] * 4, VMEM,
        (pltpu.VMEM((requests, user_proj.shape[1]), F32),),
        limit=16, flops=20_000_000, moved=1_600_000,
    )(place, cand_count, partner, user_proj, units, out_weight.reshape(1, -1))
    return (logits, pooled)


def solution(mesh):
    in_specs = (
        P(("section", "dp"), None),
        P(("section", "dp"), None, None),
        P(("section", "dp"), None, None),
        P(),
        P(None, "mp"),
        P("mp", None),
        P(),
        P("dp", None),
        P(("section", "dp", "mp"), None, None),
        P(("section", "dp", "mp"), None),
        P(("section", "dp", "mp")),
        P(),
        P(),
        P(),
        P(),
    )
    out_specs = (P(("section", "dp", "mp"), None), P(("section", "dp"), None))
    return jax.shard_map(body, mesh=mesh, in_specs=in_specs, out_specs=out_specs, check_vma=False)
```

```python
import functools
import math

import jax
import jax.numpy as jnp
from jax import lax
from jax.experimental import pallas as pl
from jax.experimental.pallas import tpu as pltpu
from jax.sharding import PartitionSpec as P

ATT = 128
CMAX = 128
HIST = 256
UP_CUTS = 4
DOWN_CUTS = 4
BF = jnp.bfloat16
F32 = jnp.float32
NT = (((1,), (1,)), ((), ()))

VMEM = pl.BlockSpec(memory_space=pltpu.VMEM)
SMEM = pl.BlockSpec(memory_space=pltpu.SMEM)
HBM = pl.BlockSpec(memory_space=pltpu.HBM)


def dot(a, b):
    return jnp.dot(a, b, preferred_element_type=F32)


def call(kernel, name, out_shape, in_specs, out_specs, scratch=(), limit=16, flops=0, moved=0):
    return pl.pallas_call(
        kernel,
        name=name,
        out_shape=out_shape,
        in_specs=in_specs,
        out_specs=out_specs,
        scratch_shapes=list(scratch),
        compiler_params=pltpu.CompilerParams(vmem_limit_bytes=limit * 2**20),
        cost_estimate=pl.CostEstimate(flops=flops, bytes_accessed=moved, transcendentals=0),
    )


def shift(value, axis, by):
    size = lax.axis_size(axis)
    return lax.ppermute(value, axis, [(i, (i + by) % size) for i in range(size)])


def swapped(value, axis, bit):
    mask = 2**bit
    pairs = [(source, source ^ mask) for source in range(lax.axis_size(axis))]
    return lax.ppermute(value, axis, pairs)


def after(value, earlier):
    return lax.optimization_barrier((value, earlier))[0]


def normalize(values, gain_row):
    squares = jnp.mean(values * values, axis=-1, keepdims=True)
    return values * lax.rsqrt(squares + 1e-06) * gain_row


def raise_rows(normed, up, act_s):
    wide = up.shape[1] // UP_CUTS
    for c in range(UP_CUTS):
        cut = slice(c * wide, (c + 1) * wide)
        act_s[:, cut] = jax.nn.gelu(dot(normed, up[:, cut])).astype(BF)


def start_kernel(
    owners, local_rows, prompt, gain, up, down,
    outgoing, target, part, prompt_v, gain_v, up_v, down_v, owners_s, local_s, act_s, sems,
):
    pairs = (
        (owners, owners_s), (local_rows, local_s), (prompt, prompt_v), (gain, gain_v),
        (up, up_v), (down, down_v),
    )
    copies = [pltpu.make_async_copy(a, b, sems.at[k]) for k, (a, b) in enumerate(pairs)]
    for copy in copies:
        copy.start()
    copies[0].wait()
    copies[1].wait()
    name_places(owners_s, local_s, outgoing, target)
    copies[2].wait()
    copies[3].wait()
    normed = normalize(prompt_v[...].astype(F32), gain_v[...]).astype(BF)
    copies[4].wait()
    raise_rows(normed, up_v, act_s)
    copies[5].wait()
    part[...] = dot(act_s[...], down_v[...]).astype(BF)


def load_kernel(up, down, up_v, down_v, sems):
    copies = [
        pltpu.make_async_copy(up, up_v, sems.at[0]),
        pltpu.make_async_copy(down, down_v, sems.at[1]),
    ]
    for copy in copies:
        copy.start()
    for copy in copies:
        copy.wait()


def lower(act_s, down, outs):
    tall = down.shape[1] // DOWN_CUTS
    own = outs[0].shape[0]
    for c in range(DOWN_CUTS):
        cut = slice(c * tall, (c + 1) * tall)
        part = dot(act_s[...], down[:, cut]).astype(BF)
        for k, out in enumerate(outs):
            out[:, cut] = part[k * own : (k + 1) * own, :]


def second_kernel(
    prompt, t0, t1, t2, t3, code_rows, gain, up, down,
    o0, o1, o2, o3, state, act_s, middle_s, normed_s,
):
    requests = prompt.shape[0]
    beams = code_rows.shape[0] // requests
    own = o0.shape[0]
    total = (
        t0[...].astype(F32) + t1[...].astype(F32) + t2[...].astype(F32) + t3[...].astype(F32)
    )
    middle = (prompt[...].astype(F32) + total).astype(BF).astype(F32)
    middle_s[0:requests, :] = middle
    middle_s[requests : 2 * requests, :] = middle
    base = lax.axis_index("mp") * (own // beams)
    for r in range(requests):
        row = middle_s[pl.ds(base + r, 1), :]
        now = (row + code_rows[r * beams : (r + 1) * beams, :].astype(F32)).astype(BF)
        if (r + 1) * beams <= own:
            state[r * beams : (r + 1) * beams, :] = now
        normed_s[r * beams : (r + 1) * beams, :] = normalize(now.astype(F32), gain[...]).astype(BF)
    raise_rows(normed_s[...], up, act_s)
    lower(act_s, down, (o0, o1, o2, o3))


def gathered(blocks, normed_s):
    own = blocks[0].shape[0]
    for k, ref in enumerate(blocks):
        normed_s[k * own : (k + 1) * own, :] = ref[...]
    return normed_s[...]


def third_kernel(n0, n1, n2, n3, up, down, o0, o1, o2, o3, act_s, normed_s):
    raise_rows(gathered((n0, n1, n2, n3), normed_s), up, act_s)
    lower(act_s, down, (o0, o1, o2, o3))


def last_kernel(n0, n1, n2, n3, pool, base, up, down, out, act_s, normed_s):
    raise_rows(gathered((n0, n1, n2, n3), normed_s), up, act_s)
    mixed = dot(pool[...], act_s[...]).astype(BF)
    out[...] = (dot(mixed, down[...]) + base[...]).astype(BF)


def advance(t0, t1, t2, t3, state, chosen, code_rows):
    total = (
        t0[...].astype(F32) + t1[...].astype(F32) + t2[...].astype(F32) + t3[...].astype(F32)
    )
    middle = (state[...].astype(F32) + total).astype(BF)
    return (dot(chosen[...], middle) + code_rows[...].astype(F32)).astype(BF)


def owner_kernel(t0, t1, t2, t3, state, chosen, code_rows, gain, out_state, out_normed):
    now = advance(t0, t1, t2, t3, state, chosen, code_rows)
    out_state[...] = now
    out_normed[...] = normalize(now.astype(F32), gain[...]).astype(BF)


def owner_last_kernel(
    t0, t1, t2, t3, state, chosen, code_rows, gain, pool, mean_code, out_base, out_normed
):
    now = advance(t0, t1, t2, t3, state, chosen, code_rows)
    out_normed[...] = normalize(now.astype(F32), gain[...]).astype(BF)
    rows = state.shape[0]
    out_base[...] = dot(pool[:, :rows], now) + mean_code[...]


def prepare_kernel(
    code, parent, table,
    rows0, rows1, rows2, mean_code, pool, chosen1, chosen2, code_s, parent_s, table_s, sems,
):
    pairs = ((code, code_s), (parent, parent_s), (table, table_s))
    copies = [pltpu.make_async_copy(a, b, sems.at[k]) for k, (a, b) in enumerate(pairs)]
    for copy in copies:
        copy.start()
    codes = table.shape[0]
    requests, _, beams = code.shape
    spots = requests * beams
    own = rows1.shape[0]
    base = lax.axis_index("mp") * (own // beams)
    row = lax.broadcasted_iota(jnp.int32, (spots, beams), 0)
    lane = lax.broadcasted_iota(jnp.int32, (spots, beams), 1)
    spread = (lane == (row // beams + base) % requests).astype(BF)
    kept = lane == row % beams

    def column(values):
        wide = dot(spread, values.astype(F32).astype(BF))
        return jnp.sum(jnp.where(kept, wide, 0.0), axis=1, keepdims=True).astype(jnp.int32)

    def picked(ids):
        names = lax.broadcasted_iota(jnp.int32, (ids.shape[0], codes), 1)
        return dot((ids == names).astype(BF), table_s[...]).astype(BF)

    copies[0].wait()
    columns = [column(code_s[:, k, :]) for k in range(3)]
    copies[1].wait()
    block = lax.broadcasted_iota(jnp.int32, (own, 1), 0) // beams * beams
    places = lax.broadcasted_iota(jnp.int32, (own, own), 1)
    for k, out in ((1, chosen1), (2, chosen2)):
        out[...] = (column(parent_s[:, k, :])[:own] + block == places).astype(BF)
    code3 = code_s[:, 3, :]
    parent3 = parent_s[:, 3, :]
    tally = jnp.zeros((requests, codes), F32)
    names = lax.broadcasted_iota(jnp.int32, (requests, codes), 1)
    kids = jnp.zeros((requests, spots), F32)
    lanes = lax.broadcasted_iota(jnp.int32, (requests, spots), 1)
    for b in range(beams):
        tally = tally + (code3[:, b : b + 1] == names).astype(F32)
        kids = kids + (parent3[:, b : b + 1] == lanes % beams).astype(F32)
    held = (base + lanes // beams) % requests
    mine = held == lax.broadcasted_iota(jnp.int32, (requests, spots), 0)
    pool[...] = jnp.where(mine, kids / beams, 0.0).astype(BF)
    number = lax.broadcasted_iota(jnp.int32, (requests, codes), 0)
    ours = (number >= base) & (number < base + own // beams)
    copies[2].wait()
    rows0[...] = picked(columns[0])
    rows1[...] = picked(columns[1][:own])
    rows2[...] = picked(columns[2][:own])
    mean_code[...] = dot(jnp.where(ours, tally / beams, 0.0).astype(BF), table_s[...])


def pool_kernel(t0, t1, t2, t3, out):
    out[...] = (
        t0[...].astype(F32) + t1[...].astype(F32) + t2[...].astype(F32) + t3[...].astype(F32)
    ).astype(BF)


def name_places(owners, local_rows, outgoing, target):
    requests, slots = local_rows.shape
    count, capacity = outgoing.shape
    before = (
        lax.broadcasted_iota(jnp.int32, (slots, slots), 0)
        < lax.broadcasted_iota(jnp.int32, (slots, slots), 1)
    ).astype(BF)
    names = lax.broadcasted_iota(jnp.int32, (count, slots), 0)
    places = lax.broadcasted_iota(jnp.int32, (128, slots), 0)
    carry = jnp.zeros((count, 1), F32)
    low = jnp.zeros((count, 128), F32)
    high = jnp.zeros((count, 128), F32)
    lines = []
    for q in range(requests):
        owner = owners[q]
        row = local_rows[q : q + 1, :]
        named = (owner == names).astype(F32)
        ahead = dot(named.astype(BF), before) + carry
        carry = carry + jnp.sum(named, axis=1, keepdims=True)
        position = jnp.sum(named * ahead, axis=0, keepdims=True).astype(jnp.int32)
        lines.append(owner * capacity + position)
        spot = (places == position).astype(BF)
        low = low + lax.dot_general(
            (named * (row & 31).astype(F32)).astype(BF), spot, NT, preferred_element_type=F32
        )
        high = high + lax.dot_general(
            (named * (row >> 5).astype(F32)).astype(BF), spot, NT, preferred_element_type=F32
        )
    outgoing[...] = (high * 32.0 + low).astype(jnp.int32)[:, :capacity]
    spare = jnp.zeros((target.shape[0] - requests, slots), jnp.int32)
    target[...] = jnp.concatenate(lines + [spare], axis=0)


def table_kernel(features, proj, table):
    table[...] = dot(features[...], proj[...]).astype(BF)


def serve_kernel(wanted, table, out, *, group):
    rows = table.shape[0]
    count, capacity, _ = out.shape
    asked = jnp.transpose(wanted[...])
    ids = lax.broadcasted_iota(jnp.int32, (capacity * group, rows), 1)
    for g in range(0, count, group):
        column = jnp.concatenate([asked[:, g + k : g + k + 1] for k in range(group)], axis=0)
        found = dot((column == ids).astype(BF), table[...]).astype(BF)
        for k in range(group):
            out[g + k] = found[k * capacity : (k + 1) * capacity, :]


def rank_kernel(target, returned, bias, user_proj, out, user_proj_v, sem):
    copy = pltpu.make_async_copy(user_proj, user_proj_v, sem)
    copy.start()
    requests = out.shape[0]
    count, capacity, width = returned.shape
    table = returned[...].reshape(count * capacity, width)
    targets = jnp.transpose(target[...])
    slots = targets.shape[0]
    ids = lax.broadcasted_iota(jnp.int32, (slots, count * capacity), 1)
    for q in range(requests):
        rows = dot((targets[:, q : q + 1] == ids).astype(BF), table).astype(BF)
        queries = rows[:CMAX, :ATT]
        keys = rows[CMAX:, :ATT]
        scores = lax.dot_general(queries, keys, NT, preferred_element_type=F32) / math.sqrt(ATT)
        weights = jax.nn.sigmoid(scores).astype(BF)
        interest = dot(weights, rows[CMAX:, ATT:]) / math.sqrt(HIST)
        out[q] = interest + rows[:CMAX, ATT:].astype(F32) + bias[...]
    copy.wait()


def logit_kernel(counts, users, user_proj, units, weight, out, term_s):
    term_s[...] = dot(users[...], user_proj[...])
    requests = units.shape[0]
    base = lax.axis_index("mp") * requests
    lanes = lax.broadcasted_iota(jnp.int32, (1, CMAX), 1)
    for q in range(requests):
        hidden = jnp.maximum(units[q] + term_s[pl.ds(base + q, 1), :], 0.0)
        line = lax.dot_general(
            weight[...], hidden, NT, preferred_element_type=F32, precision=lax.Precision.HIGHEST
        )
        out[q : q + 1, :] = jnp.where(lanes < counts[q], line, 0.0)


def body(
    prompt_state,
    beam_parent,
    beam_code,
    norm_gain,
    up_weight,
    down_weight,
    code_table,
    item_features,
    lookup_owner,
    lookup_row,
    cand_count,
    item_proj,
    user_proj,
    rank_bias,
    out_weight,
):
    requests, width = prompt_state.shape
    beams = beam_parent.shape[2]
    hidden = up_weight.shape[1]
    rows = requests * beams
    rank_rows, slots = lookup_row.shape
    own = rank_rows * beams
    owner_count = lax.axis_size("dp")
    capacity = max(2, 2 * rank_rows * slots // owner_count)
    columns = item_proj.shape[1]
    gain = norm_gain.reshape(1, width)
    shape = jax.ShapeDtypeStruct
    DMA = pltpu.SemaphoreType.DMA

    outgoing, target, part, prompt, gain, up, down = call(
        start_kernel, "start",
        (
            shape((owner_count, capacity), jnp.int32), shape((8, slots), jnp.int32),
            shape((requests, width), BF), shape((requests, width), BF), shape((1, width), F32),
            shape((width, hidden), BF), shape((hidden, width), BF),
        ),
        [HBM] * 6, (VMEM,) * 7,
        (
            pltpu.VMEM((rank_rows, 1, slots), jnp.int32), pltpu.VMEM((rank_rows, slots), jnp.int32),
            pltpu.VMEM((requests, hidden), BF), DMA((6,)),
        ),
        limit=40, flops=100 * rows * width * hidden, moved=1_000_000,
    )(
        jnp.transpose(lookup_owner, (0, 2, 1)), lookup_row, prompt_state, gain,
        up_weight, down_weight,
    )
    parts = [shift(part, "mp", k) for k in (1, 2, 3)]
    began = part
    rows0, rows1, rows2, mean_code, pool, chosen1, chosen2 = call(
        prepare_kernel, "prepare",
        (
            shape((rows, width), BF), shape((own, width), BF), shape((own, width), BF),
            shape((requests, width), F32), shape((requests, rows), BF),
            shape((own, own), BF), shape((own, own), BF),
        ),
        [HBM] * 3, (VMEM,) * 7,
        (
            pltpu.VMEM(beam_code.shape, jnp.int32), pltpu.VMEM(beam_parent.shape, jnp.int32),
            pltpu.VMEM(code_table.shape, BF), DMA((3,)),
        ),
        limit=16, flops=2 * 400 * 256 * width, moved=3_000_000,
    )(beam_code, after(beam_parent, part), code_table)
    ffn = dict(limit=16, flops=4 * rows * width * hidden, moved=50 * width * hidden)

    quarter = (shape((own, width), BF),) * 4
    *outs, state = call(
        second_kernel, "ffn1", quarter + (shape((own, width), BF),),
        [VMEM] * 9, (VMEM,) * 5,
        (pltpu.VMEM((rows, hidden), BF),
         pltpu.VMEM((2 * requests, width), F32), pltpu.VMEM((rows, width), BF)),
        **ffn,
    )(prompt, part, *parts, rows0, gain, up, down)
    outgoing = after(outgoing, outs[0])
    wanted = lax.all_to_all(outgoing, "dp", split_axis=0, concat_axis=0, tiled=True)
    sums = [outs[0]] + [shift(outs[k], "mp", k) for k in (1, 2, 3)]
    state, normed = call(
        owner_kernel, "owner1", (shape((own, width), BF),) * 2, [VMEM] * 8, (VMEM,) * 2,
        limit=16, flops=2 * own * own * width, moved=2_000_000,
    )(*sums, state, chosen1, rows1, gain)

    up, down = call(
        load_kernel, "load", (shape((width, hidden), BF), shape((hidden, width), BF)),
        [HBM] * 2, (VMEM,) * 2, (DMA((2,)),), limit=40, flops=20 * rows * width * hidden, moved=1_000_000,
    )(after(up_weight, normed), after(down_weight, normed))
    wanted = after(wanted, normed)
    others = [normed] + [shift(normed, "mp", -k) for k in (1, 2, 3)]
    outs = call(
        third_kernel, "ffn2", quarter, [VMEM] * 6, (VMEM,) * 4,
        (pltpu.VMEM((rows, hidden), BF), pltpu.VMEM((rows, width), BF)),
        **ffn,
    )(*others, up, down)
    sums = [outs[0]] + [shift(outs[k], "mp", k) for k in (1, 2, 3)]
    base, normed = call(
        owner_last_kernel, "owner2", (shape((requests, width), F32), shape((own, width), BF)),
        [VMEM] * 10, (VMEM,) * 2,
        limit=16, flops=2 * own * own * width, moved=2_000_000,
    )(*sums, state, chosen2, rows2, gain, pool, mean_code)

    others = [normed] + [shift(normed, "mp", -k) for k in (1, 2, 3)]
    part = call(
        last_kernel, "ffn3", shape((requests, width), BF), [VMEM] * 8, VMEM,
        (pltpu.VMEM((rows, hidden), BF), pltpu.VMEM((rows, width), BF)),
        **ffn,
    )(*others, pool, base, up, down)
    parts = [shift(part, "mp", k) for k in (1, 2, 3)]
    table = call(
        table_kernel, "table", shape((item_features.shape[0], columns), BF), [VMEM] * 2, VMEM,
        limit=16, flops=2 * item_features.size * columns, moved=4_000_000,
    )(item_features, after(item_proj, began))
    served = call(
        functools.partial(serve_kernel, group=4), "serve",
        shape((owner_count, capacity, columns), BF), [VMEM] * 2, VMEM, limit=16,
        flops=2 * owner_count * capacity * item_features.shape[0] * columns, moved=4_000_000,
    )(wanted, table)
    returned = lax.all_to_all(served, "dp", split_axis=0, concat_axis=0, tiled=True)
    returned = after(returned, part)
    units, user_proj = call(
        rank_kernel, "rank",
        (shape((rank_rows, CMAX, columns - ATT), F32), shape(user_proj.shape, BF)),
        [VMEM] * 3 + [HBM], (VMEM,) * 2, (DMA,), limit=16,
        flops=2 * rank_rows * slots * owner_count * capacity * columns, moved=4_000_000,
    )(target, returned, rank_bias.reshape(1, -1), user_proj)
    part_late = after(part, units)
    pooled = call(
        pool_kernel, "pool", shape((requests, width), BF), [VMEM] * 4, VMEM,
        limit=16, flops=100_000, moved=400_000,
    )(part_late, *parts)
    partner = swapped(pooled, "section", 0)

    logits = call(
        logit_kernel, "logit", shape((rank_rows, CMAX), F32), [SMEM] + [VMEM] * 4, VMEM,
        (pltpu.VMEM((requests, user_proj.shape[1]), F32),),
        limit=16, flops=20_000_000, moved=1_600_000,
    )(cand_count, partner, user_proj, units, out_weight.reshape(1, -1))
    return (logits, pooled)


def solution(mesh):
    in_specs = (
        P(("section", "dp"), None),
        P(("section", "dp"), None, None),
        P(("section", "dp"), None, None),
        P(),
        P(None, "mp"),
        P("mp", None),
        P(),
        P("dp", None),
        P(("section", "dp", "mp"), None, None),
        P(("section", "dp", "mp"), None),
        P(("section", "dp", "mp")),
        P(),
        P(),
        P(),
        P(),
    )
    out_specs = (P(("section", "dp", "mp"), None), P(("section", "dp"), None))
    return jax.shard_map(body, mesh=mesh, in_specs=in_specs, out_specs=out_specs, check_vma=False)
```

```python
import functools
import math

import jax
import jax.numpy as jnp
from jax import lax
from jax.experimental import pallas as pl
from jax.experimental.pallas import tpu as pltpu
from jax.sharding import PartitionSpec as P

ATT = 128
CMAX = 128
HIST = 256
UP_CUTS = 4
DOWN_CUTS = 4
BF = jnp.bfloat16
F32 = jnp.float32
NT = (((1,), (1,)), ((), ()))
RING = 4

VMEM = pl.BlockSpec(memory_space=pltpu.VMEM)
SMEM = pl.BlockSpec(memory_space=pltpu.SMEM)
HBM = pl.BlockSpec(memory_space=pltpu.HBM)


def dot(a, b):
    return jnp.dot(a, b, preferred_element_type=F32)


def call(kernel, name, out_shape, in_specs, out_specs, scratch=(), limit=16, flops=0, moved=0):
    return pl.pallas_call(
        kernel,
        name=name,
        out_shape=out_shape,
        in_specs=in_specs,
        out_specs=out_specs,
        scratch_shapes=list(scratch),
        compiler_params=pltpu.CompilerParams(vmem_limit_bytes=limit * 2**20),
        cost_estimate=pl.CostEstimate(flops=flops, bytes_accessed=moved, transcendentals=0),
    )


def shift(value, axis, by):
    size = lax.axis_size(axis)
    return lax.ppermute(value, axis, [(i, (i + by) % size) for i in range(size)])


def swapped(value, axis, bit):
    mask = 2**bit
    pairs = [(source, source ^ mask) for source in range(lax.axis_size(axis))]
    return lax.ppermute(value, axis, pairs)


def after(value, earlier):
    return lax.optimization_barrier((value, earlier))[0]


def normalize(values, gain_row):
    squares = jnp.mean(values * values, axis=-1, keepdims=True)
    return values * lax.rsqrt(squares + 1e-06) * gain_row


def raise_rows(normed, up, act_s):
    wide = up.shape[1] // UP_CUTS
    for c in range(UP_CUTS):
        cut = slice(c * wide, (c + 1) * wide)
        act_s[:, cut] = jax.nn.gelu(dot(normed, up[:, cut])).astype(BF)


def start_kernel(prompt, gain, up, down, part, prompt_v, gain_v, up_v, down_v, act_s, sems):
    pairs = ((prompt, prompt_v), (gain, gain_v), (up, up_v), (down, down_v))
    copies = [pltpu.make_async_copy(a, b, sems.at[k]) for k, (a, b) in enumerate(pairs)]
    for copy in copies:
        copy.start()
    copies[0].wait()
    copies[1].wait()
    normed = normalize(prompt_v[...].astype(F32), gain_v[...]).astype(BF)
    copies[2].wait()
    raise_rows(normed, up_v, act_s)
    copies[3].wait()
    part[...] = dot(act_s[...], down_v[...]).astype(BF)


def lower(act_s, down, outs):
    tall = down.shape[1] // DOWN_CUTS
    own = outs[0].shape[0]
    for c in range(DOWN_CUTS):
        cut = slice(c * tall, (c + 1) * tall)
        part = dot(act_s[...], down[:, cut]).astype(BF)
        for k, out in enumerate(outs):
            out[:, cut] = part[k * own : (k + 1) * own, :]


def second_kernel(
    prompt, t0, t1, t2, t3, code_rows, gain, up, down,
    o0, o1, o2, o3, state, act_s, middle_s, normed_s,
):
    requests = prompt.shape[0]
    beams = code_rows.shape[0] // requests
    own = o0.shape[0]
    total = (
        t0[...].astype(F32) + t1[...].astype(F32) + t2[...].astype(F32) + t3[...].astype(F32)
    )
    middle = (prompt[...].astype(F32) + total).astype(BF).astype(F32)
    middle_s[0:requests, :] = middle
    middle_s[requests : 2 * requests, :] = middle
    base = lax.axis_index("mp") * (own // beams)
    for r in range(requests):
        row = middle_s[pl.ds(base + r, 1), :]
        now = (row + code_rows[r * beams : (r + 1) * beams, :].astype(F32)).astype(BF)
        if (r + 1) * beams <= own:
            state[r * beams : (r + 1) * beams, :] = now
        normed_s[r * beams : (r + 1) * beams, :] = normalize(now.astype(F32), gain[...]).astype(BF)
    raise_rows(normed_s[...], up, act_s)
    lower(act_s, down, (o0, o1, o2, o3))


def gathered(blocks, normed_s):
    first = 0
    for ref in blocks:
        normed_s[first : first + ref.shape[0], :] = ref[...]
        first += ref.shape[0]
    return normed_s[...]


def third_kernel(*refs):
    *blocks, up, down, o0, o1, o2, o3, act_s, normed_s = refs
    raise_rows(gathered(blocks, normed_s), up, act_s)
    lower(act_s, down, (o0, o1, o2, o3))


def last_kernel(*refs):
    *blocks, pool, base, up, down, out, act_s, normed_s = refs
    raise_rows(gathered(blocks, normed_s), up, act_s)
    mixed = dot(pool[...], act_s[...]).astype(BF)
    out[...] = (dot(mixed, down[...]) + base[...]).astype(BF)


def halves_kernel(before, behind, top, bottom):
    rows = top.shape[0]
    top[...] = before[:rows, :]
    bottom[...] = behind[rows:, :]


def advance(t0, t1, t2, t3, state, chosen, code_rows):
    total = (
        t0[...].astype(F32) + t1[...].astype(F32) + t2[...].astype(F32) + t3[...].astype(F32)
    )
    middle = (state[...].astype(F32) + total).astype(BF)
    return (dot(chosen[...], middle) + code_rows[...].astype(F32)).astype(BF)


def owner_kernel(t0, t1, t2, t3, state, chosen, code_rows, gain, out_state, out_normed):
    now = advance(t0, t1, t2, t3, state, chosen, code_rows)
    out_state[...] = now
    out_normed[...] = normalize(now.astype(F32), gain[...]).astype(BF)


def owner_last_kernel(
    t0, t1, t2, t3, state, chosen, code_rows, gain, pool, mean_code, out_base, out_normed
):
    now = advance(t0, t1, t2, t3, state, chosen, code_rows)
    out_normed[...] = normalize(now.astype(F32), gain[...]).astype(BF)
    rows = state.shape[0]
    out_base[...] = dot(pool[:, :rows], now) + mean_code[...]


def prepare_kernel(
    code, parent, table,
    rows0, rows1, rows2, mean_code, pool, chosen1, chosen2, code_s, parent_s, table_s, sems,
):
    pairs = ((code, code_s), (parent, parent_s), (table, table_s))
    copies = [pltpu.make_async_copy(a, b, sems.at[k]) for k, (a, b) in enumerate(pairs)]
    for copy in copies:
        copy.start()
    codes = table.shape[0]
    requests, _, beams = code.shape
    spots = requests * beams
    own = rows1.shape[0]
    base = lax.axis_index("mp") * (own // beams)
    row = lax.broadcasted_iota(jnp.int32, (spots, beams), 0)
    lane = lax.broadcasted_iota(jnp.int32, (spots, beams), 1)
    spread = (lane == (row // beams + base) % requests).astype(BF)
    kept = lane == row % beams

    def column(values):
        wide = dot(spread, values.astype(F32).astype(BF))
        return jnp.sum(jnp.where(kept, wide, 0.0), axis=1, keepdims=True).astype(jnp.int32)

    def picked(ids):
        names = lax.broadcasted_iota(jnp.int32, (ids.shape[0], codes), 1)
        return dot((ids == names).astype(BF), table_s[...]).astype(BF)

    copies[0].wait()
    columns = [column(code_s[:, k, :]) for k in range(3)]
    copies[1].wait()
    block = lax.broadcasted_iota(jnp.int32, (own, 1), 0) // beams * beams
    places = lax.broadcasted_iota(jnp.int32, (own, own), 1)
    for k, out in ((1, chosen1), (2, chosen2)):
        out[...] = (column(parent_s[:, k, :])[:own] + block == places).astype(BF)
    code3 = code_s[:, 3, :]
    parent3 = parent_s[:, 3, :]
    tally = jnp.zeros((requests, codes), F32)
    names = lax.broadcasted_iota(jnp.int32, (requests, codes), 1)
    kids = jnp.zeros((requests, spots), F32)
    lanes = lax.broadcasted_iota(jnp.int32, (requests, spots), 1)
    for b in range(beams):
        tally = tally + (code3[:, b : b + 1] == names).astype(F32)
        kids = kids + (parent3[:, b : b + 1] == lanes % beams).astype(F32)
    held = (base + lanes // beams) % requests
    mine = held == lax.broadcasted_iota(jnp.int32, (requests, spots), 0)
    pool[...] = jnp.where(mine, kids / beams, 0.0).astype(BF)
    number = lax.broadcasted_iota(jnp.int32, (requests, codes), 0)
    ours = (number >= base) & (number < base + own // beams)
    copies[2].wait()
    rows0[...] = picked(columns[0])
    rows1[...] = picked(columns[1][:own])
    rows2[...] = picked(columns[2][:own])
    mean_code[...] = dot(jnp.where(ours, tally / beams, 0.0).astype(BF), table_s[...])


def pool_kernel(t0, t1, t2, t3, out):
    out[...] = (
        t0[...].astype(F32) + t1[...].astype(F32) + t2[...].astype(F32) + t3[...].astype(F32)
    ).astype(BF)


def index_kernel(owners, local_rows, ask0, ask1, ask2, ask3, target, asked_s):
    asks = (ask0, ask1, ask2, ask3)
    requests, slots = local_rows.shape
    deep, capacity = asks[0].shape
    count = deep * RING
    here = lax.axis_index("dp") % RING
    before = (
        lax.broadcasted_iota(jnp.int32, (slots, slots), 0)
        < lax.broadcasted_iota(jnp.int32, (slots, slots), 1)
    ).astype(BF)
    names = lax.broadcasted_iota(jnp.int32, (count, slots), 0)
    places = lax.broadcasted_iota(jnp.int32, (128, slots), 0)
    carry = jnp.zeros((count, 1), F32)
    low = jnp.zeros((count, 128), F32)
    high = jnp.zeros((count, 128), F32)
    lines = []
    for q in range(requests):
        owner = owners[q]
        row = local_rows[q : q + 1, :]
        named = (owner == names).astype(F32)
        ahead = dot(named.astype(BF), before) + carry
        carry = carry + jnp.sum(named, axis=1, keepdims=True)
        position = jnp.sum(named * ahead, axis=0, keepdims=True).astype(jnp.int32)
        away = (owner - here + RING) % RING
        lines.append((away * deep + owner // RING) * capacity + position)
        spot = (places == position).astype(BF)
        low = low + lax.dot_general(
            (named * (row & 31).astype(F32)).astype(BF), spot, NT, preferred_element_type=F32
        )
        high = high + lax.dot_general(
            (named * (row >> 5).astype(F32)).astype(BF), spot, NT, preferred_element_type=F32
        )
    asked_s[...] = (high * 32.0 + low).astype(jnp.int32)
    for k, ask in enumerate(asks):
        there = (here + k) % RING
        for z in range(deep):
            ask[z : z + 1, :] = asked_s[pl.ds(z * RING + there, 1), :][:, :capacity]
    spare = jnp.zeros((target.shape[0] - requests, slots), jnp.int32)
    target[...] = jnp.concatenate(lines + [spare], axis=0)


def table_kernel(features, proj, table, features_s, proj_s, sems):
    rows = table.shape[0]
    first = lax.axis_index("section") * rows
    copies = [
        pltpu.make_async_copy(features.at[pl.ds(first, rows)], features_s, sems.at[0]),
        pltpu.make_async_copy(proj, proj_s, sems.at[1]),
    ]
    for copy in copies:
        copy.start()
    for copy in copies:
        copy.wait()
    table[...] = dot(features_s[...], proj_s[...]).astype(BF)


def serve_kernel(ask0, ask1, ask2, ask3, table, out0, out1, out2, out3, table_s, sems):
    outs = (out0, out1, out2, out3)
    deep, capacity = ask0.shape
    rows = table_s.shape[1]
    copies = [
        pltpu.make_async_copy(table.at[pl.ds(z * rows, rows)], table_s.at[z], sems.at[z])
        for z in range(deep)
    ]
    for copy in copies[:4]:
        copy.start()
    turned = [jnp.transpose(ask[...]) for ask in (ask0, ask1, ask2, ask3)]
    ids = lax.broadcasted_iota(jnp.int32, (capacity * RING, rows), 1)
    for z in range(deep):
        column = jnp.concatenate([value[:, z : z + 1] for value in turned], axis=0)
        copies[z].wait()
        if z + 4 < deep:
            copies[z + 4].start()
        found = dot((column == ids).astype(BF), table_s[z]).astype(BF)
        for k, out in enumerate(outs):
            out[z * capacity : (z + 1) * capacity, :] = found[k * capacity : (k + 1) * capacity, :]


def found_rows(targets, q, first, part):
    column = targets[:, q : q + 1] - first
    ids = lax.broadcasted_iota(jnp.int32, (targets.shape[0], part.shape[0]), 1)
    return dot((column == ids).astype(BF), part[...])


def pick_kernel(target, part, out, *, first):
    targets = jnp.transpose(target[...])
    for q in range(out.shape[0]):
        out[q] = found_rows(targets, q, first, part).astype(BF)


def pick_more_kernel(target, rows, part, out, *, first):
    targets = jnp.transpose(target[...])
    for q in range(out.shape[0]):
        out[q] = rows[q] + found_rows(targets, q, first, part).astype(BF)


def rank_kernel(target, rows, part, bias, user_proj, out, user_proj_v, sem, *, first):
    copy = pltpu.make_async_copy(user_proj, user_proj_v, sem)
    copy.start()
    targets = jnp.transpose(target[...])
    for q in range(out.shape[0]):
        held = rows[q] + found_rows(targets, q, first, part).astype(BF)
        queries = held[:CMAX, :ATT]
        keys = held[CMAX:, :ATT]
        scores = lax.dot_general(queries, keys, NT, preferred_element_type=F32) / math.sqrt(ATT)
        weights = jax.nn.sigmoid(scores).astype(BF)
        interest = dot(weights, held[CMAX:, ATT:]) / math.sqrt(HIST)
        out[q] = jnp.transpose(interest + held[:CMAX, ATT:].astype(F32) + bias[...])
    copy.wait()


def logit_kernel(counts, users, user_proj, units, weight, out):
    requests, values, _ = units.shape
    terms = jnp.transpose(dot(users[...], user_proj[...]))
    base = lax.axis_index("mp") * requests
    rows = lax.broadcasted_iota(jnp.int32, terms.shape, 1)
    lanes = lax.broadcasted_iota(jnp.int32, (1, CMAX), 1)
    scale = jnp.transpose(jnp.broadcast_to(weight[...], (8, values)))[:, :1]
    for q in range(requests):
        term = jnp.sum(jnp.where(rows == base + q, terms, 0.0), axis=1, keepdims=True)
        hidden = jnp.maximum(units[q] + term, 0.0) * scale
        line = jnp.sum(hidden, axis=0, keepdims=True)
        out[q : q + 1, :] = jnp.where(lanes < counts[q], line, 0.0)


def body(
    prompt_state,
    beam_parent,
    beam_code,
    norm_gain,
    up_weight,
    down_weight,
    code_table,
    item_features,
    lookup_owner,
    lookup_row,
    cand_count,
    item_proj,
    user_proj,
    rank_bias,
    out_weight,
):
    requests, width = prompt_state.shape
    beams = beam_parent.shape[2]
    hidden = up_weight.shape[1]
    rows = requests * beams
    rank_rows, slots = lookup_row.shape
    own = rank_rows * beams
    owner_count = lax.axis_size("dp")
    capacity = max(2, 2 * rank_rows * slots // owner_count)
    columns = item_proj.shape[1]
    gain = norm_gain.reshape(1, width)
    shape = jax.ShapeDtypeStruct
    DMA = pltpu.SemaphoreType.DMA

    deep = owner_count // RING
    items = item_features.shape[0]
    half = items // lax.axis_size("section")
    table = call(
        table_kernel, "table", shape((half, columns), BF), [HBM] * 2, VMEM,
        (
            pltpu.VMEM((half, item_features.shape[1]), BF), pltpu.VMEM(item_proj.shape, BF),
            DMA((2,)),
        ),
        limit=60, flops=2 * half * item_proj.size, moved=2_000_000,
    )(item_features, item_proj)
    mine = lax.all_gather(
        table, ("section", "dp"), tiled=True,
        axis_index_groups=[
            [s * owner_count + z * RING + x for z in range(deep) for s in range(items // half)]
            for x in range(RING)
        ],
    )

    part, prompt, gain, up, down = call(
        start_kernel, "start",
        (
            shape((requests, width), BF), shape((requests, width), BF), shape((1, width), F32),
            shape((width, hidden), BF), shape((hidden, width), BF),
        ),
        [HBM] * 4, (VMEM,) * 5, (pltpu.VMEM((requests, hidden), BF), DMA((4,))),
        limit=40, flops=100 * rows * width * hidden, moved=1_000_000,
    )(after(prompt_state, table), gain, up_weight, down_weight)
    parts = [shift(part, "mp", k) for k in (1, 2, 3)]

    def shared(normed, ringed):
        if not ringed:
            return [normed] + [shift(normed, "mp", -k) for k in (1, 2, 3)]
        behind, before = shift(normed, "mp", -1), shift(normed, "mp", 1)
        top, bottom = call(
            halves_kernel, "halves", (shape((own // 2, width), BF),) * 2, [VMEM] * 2, (VMEM,) * 2,
            limit=16, flops=1000, moved=1_000_000,
        )(before, behind)
        return [normed, behind, shift(top, "mp", 1), shift(bottom, "mp", -1), before]

    def along(value, by):
        pairs = [
            (z * RING + x, z * RING + (x + by) % RING) for z in range(deep) for x in range(RING)
        ]
        return lax.ppermute(value, "dp", pairs)

    rows0, rows1, rows2, mean_code, pool, chosen1, chosen2 = call(
        prepare_kernel, "prepare",
        (
            shape((rows, width), BF), shape((own, width), BF), shape((own, width), BF),
            shape((requests, width), F32), shape((requests, rows), BF),
            shape((own, own), BF), shape((own, own), BF),
        ),
        [HBM] * 3, (VMEM,) * 7,
        (
            pltpu.VMEM(beam_code.shape, jnp.int32), pltpu.VMEM(beam_parent.shape, jnp.int32),
            pltpu.VMEM(code_table.shape, BF), DMA((3,)),
        ),
        limit=16, flops=2 * 400 * 256 * width, moved=3_000_000,
    )(beam_code, after(beam_parent, part), code_table)
    ffn = dict(limit=16, flops=4 * rows * width * hidden, moved=50 * width * hidden)

    quarter = (shape((own, width), BF),) * 4
    *outs, state = call(
        second_kernel, "ffn1", quarter + (shape((own, width), BF),),
        [VMEM] * 9, (VMEM,) * 5,
        (pltpu.VMEM((rows, hidden), BF),
         pltpu.VMEM((2 * requests, width), F32), pltpu.VMEM((rows, width), BF)),
        **ffn,
    )(prompt, part, *parts, rows0, gain, up, down)
    ask0, ask1, ask2, ask3, target = call(
        index_kernel, "index",
        (shape((deep, capacity), jnp.int32),) * RING + (shape((8, slots), jnp.int32),),
        [VMEM] * 2, (VMEM,) * 5, (pltpu.VMEM((owner_count, 128), jnp.int32),),
        limit=16, flops=200_000_000, moved=100_000,
    )(jnp.transpose(lookup_owner, (0, 2, 1)), after(lookup_row, outs[0]))
    wanted = [ask0] + [along(after(a, outs[0]), k) for k, a in ((1, ask1), (2, ask2), (3, ask3))]
    sums = [outs[0]] + [shift(outs[k], "mp", k) for k in (1, 2, 3)]
    state, normed = call(
        owner_kernel, "owner1", (shape((own, width), BF),) * 2, [VMEM] * 8, (VMEM,) * 2,
        limit=16, flops=2 * own * own * width, moved=2_000_000,
    )(*sums, state, after(chosen1, wanted), rows1, gain)

    others = shared(normed, True)
    outs = call(
        third_kernel, "ffn2", quarter, [VMEM] * (len(others) + 2), (VMEM,) * 4,
        (pltpu.VMEM((rows, hidden), BF), pltpu.VMEM((rows, width), BF)),
        **ffn,
    )(*others, up, down)
    sums = [outs[0]] + [shift(outs[k], "mp", k) for k in (1, 2, 3)]
    mine = after(mine, outs[0])
    served = call(
        serve_kernel, "serve", (shape((deep * capacity, columns), BF),) * RING,
        [VMEM] * RING + [HBM], (VMEM,) * RING,
        (pltpu.VMEM((deep, items, columns), BF), DMA((deep,))),
        limit=46, flops=2 * owner_count * capacity * items * columns, moved=8_000_000,
    )(*wanted, mine)
    returned = [served[0]] + [along(served[k], -k) for k in (1, 2, 3)]
    base, normed = call(
        owner_last_kernel, "owner2", (shape((requests, width), F32), shape((own, width), BF)),
        [VMEM] * 10, (VMEM,) * 2,
        limit=16, flops=2 * own * own * width, moved=2_000_000,
    )(*sums, state, after(chosen2, served[0]), rows2, gain, pool, mean_code)

    others = shared(normed, True)
    part = call(
        last_kernel, "ffn3", shape((requests, width), BF), [VMEM] * (len(others) + 4), VMEM,
        (pltpu.VMEM((rows, hidden), BF), pltpu.VMEM((rows, width), BF)),
        **ffn,
    )(*others, pool, base, up, down)
    parts = [shift(part, "mp", k) for k in (1, 2, 3)]
    block = deep * capacity
    pick = dict(limit=16, flops=2 * rank_rows * slots * block * columns, moved=2_000_000)
    picked = shape((rank_rows, slots, columns), BF)
    picks = call(
        functools.partial(pick_kernel, first=0), "pick0", picked, [VMEM] * 2, VMEM, **pick
    )(target, returned[0])
    for k in (1, 3):
        picks = call(
            functools.partial(pick_more_kernel, first=k * block), f"pick{k}",
            picked, [VMEM] * 3, VMEM, **pick,
        )(target, picks, after(returned[k], part))
    units, user_proj = call(
        functools.partial(rank_kernel, first=2 * block), "rank",
        (shape((rank_rows, columns - ATT, CMAX), F32), shape(user_proj.shape, BF)),
        [VMEM] * 4 + [HBM], (VMEM,) * 2, (DMA,), **pick,
    )(target, picks, after(returned[2], part), rank_bias.reshape(1, -1), user_proj)
    pooled = call(
        pool_kernel, "pool", shape((requests, width), BF), [VMEM] * 4, VMEM,
        limit=16, flops=100_000, moved=400_000,
    )(part, *parts)
    partner = swapped(pooled, "section", 0)

    logits = call(
        logit_kernel, "logit", shape((rank_rows, CMAX), F32), [SMEM] + [VMEM] * 4, VMEM,
        limit=16, flops=20_000_000, moved=1_600_000,
    )(cand_count, partner, user_proj, units, out_weight.reshape(1, -1))
    return (logits, pooled)


def solution(mesh):
    in_specs = (
        P(("section", "dp"), None),
        P(("section", "dp"), None, None),
        P(("section", "dp"), None, None),
        P(),
        P(None, "mp"),
        P("mp", None),
        P(),
        P("dp", None),
        P(("section", "dp", "mp"), None, None),
        P(("section", "dp", "mp"), None),
        P(("section", "dp", "mp")),
        P(),
        P(),
        P(),
        P(),
    )
    out_specs = (P(("section", "dp", "mp"), None), P(("section", "dp"), None))
    return jax.shard_map(body, mesh=mesh, in_specs=in_specs, out_specs=out_specs, check_vma=False)
```

```python
import functools
import math

import jax
import jax.numpy as jnp
from jax import lax
from jax.experimental import pallas as pl
from jax.experimental.pallas import tpu as pltpu
from jax.sharding import PartitionSpec as P

ATT = 128
CMAX = 128
HIST = 256
UP_CUTS = 4
DOWN_CUTS = 4
BF = jnp.bfloat16
F32 = jnp.float32
NT = (((1,), (1,)), ((), ()))

VMEM = pl.BlockSpec(memory_space=pltpu.VMEM)
SMEM = pl.BlockSpec(memory_space=pltpu.SMEM)
HBM = pl.BlockSpec(memory_space=pltpu.HBM)


def dot(a, b):
    return jnp.dot(a, b, preferred_element_type=F32)


def call(kernel, name, out_shape, in_specs, out_specs, scratch=(), limit=16, flops=0, moved=0):
    return pl.pallas_call(
        kernel,
        name=name,
        out_shape=out_shape,
        in_specs=in_specs,
        out_specs=out_specs,
        scratch_shapes=list(scratch),
        compiler_params=pltpu.CompilerParams(vmem_limit_bytes=limit * 2**20),
        cost_estimate=pl.CostEstimate(flops=flops, bytes_accessed=moved, transcendentals=0),
    )


def shift(value, axis, by):
    size = lax.axis_size(axis)
    return lax.ppermute(value, axis, [(i, (i + by) % size) for i in range(size)])


def swapped(value, axis, bit):
    mask = 2**bit
    pairs = [(source, source ^ mask) for source in range(lax.axis_size(axis))]
    return lax.ppermute(value, axis, pairs)


def after(value, earlier):
    return lax.optimization_barrier((value, earlier))[0]


def normalize(values, gain_row):
    squares = jnp.mean(values * values, axis=-1, keepdims=True)
    return values * lax.rsqrt(squares + 1e-06) * gain_row


def raise_rows(normed, up, act_s):
    wide = up.shape[1] // UP_CUTS
    for c in range(UP_CUTS):
        cut = slice(c * wide, (c + 1) * wide)
        act_s[:, cut] = jax.nn.gelu(dot(normed, up[:, cut])).astype(BF)


def start_kernel(
    owners, local_rows, prompt, gain, up, down,
    outgoing, target, part, prompt_v, gain_v, up_v, down_v, owners_s, local_s, act_s, sems,
):
    pairs = (
        (owners, owners_s), (local_rows, local_s), (prompt, prompt_v), (gain, gain_v),
        (up, up_v), (down, down_v),
    )
    copies = [pltpu.make_async_copy(a, b, sems.at[k]) for k, (a, b) in enumerate(pairs)]
    for copy in copies:
        copy.start()
    copies[0].wait()
    copies[1].wait()
    name_places(owners_s, local_s, outgoing, target)
    copies[2].wait()
    copies[3].wait()
    normed = normalize(prompt_v[...].astype(F32), gain_v[...]).astype(BF)
    copies[4].wait()
    raise_rows(normed, up_v, act_s)
    copies[5].wait()
    part[...] = dot(act_s[...], down_v[...]).astype(BF)


def load_kernel(up, down, up_v, down_v, sems):
    copies = [
        pltpu.make_async_copy(up, up_v, sems.at[0]),
        pltpu.make_async_copy(down, down_v, sems.at[1]),
    ]
    for copy in copies:
        copy.start()
    for copy in copies:
        copy.wait()


def lower(act_s, down, outs):
    tall = down.shape[1] // DOWN_CUTS
    own = outs[0].shape[0]
    for c in range(DOWN_CUTS):
        cut = slice(c * tall, (c + 1) * tall)
        part = dot(act_s[...], down[:, cut]).astype(BF)
        for k, out in enumerate(outs):
            out[:, cut] = part[k * own : (k + 1) * own, :]


def second_kernel(
    prompt, t0, t1, t2, t3, code_rows, gain, up, down,
    o0, o1, o2, o3, state, act_s, middle_s, normed_s,
):
    requests = prompt.shape[0]
    beams = code_rows.shape[0] // requests
    own = o0.shape[0]
    total = (
        t0[...].astype(F32) + t1[...].astype(F32) + t2[...].astype(F32) + t3[...].astype(F32)
    )
    middle = (prompt[...].astype(F32) + total).astype(BF).astype(F32)
    middle_s[0:requests, :] = middle
    middle_s[requests : 2 * requests, :] = middle
    base = lax.axis_index("mp") * (own // beams)
    for r in range(requests):
        row = middle_s[pl.ds(base + r, 1), :]
        now = (row + code_rows[r * beams : (r + 1) * beams, :].astype(F32)).astype(BF)
        if (r + 1) * beams <= own:
            state[r * beams : (r + 1) * beams, :] = now
        normed_s[r * beams : (r + 1) * beams, :] = normalize(now.astype(F32), gain[...]).astype(BF)
    raise_rows(normed_s[...], up, act_s)
    lower(act_s, down, (o0, o1, o2, o3))


def gathered(blocks, normed_s):
    first = 0
    for ref in blocks:
        normed_s[first : first + ref.shape[0], :] = ref[...]
        first += ref.shape[0]
    return normed_s[...]


def third_kernel(*refs):
    *blocks, up, down, o0, o1, o2, o3, act_s, normed_s = refs
    raise_rows(gathered(blocks, normed_s), up, act_s)
    lower(act_s, down, (o0, o1, o2, o3))


def last_kernel(*refs):
    *blocks, pool, base, up, down, out, act_s, normed_s = refs
    raise_rows(gathered(blocks, normed_s), up, act_s)
    mixed = dot(pool[...], act_s[...]).astype(BF)
    out[...] = (dot(mixed, down[...]) + base[...]).astype(BF)


def halves_kernel(before, behind, top, bottom):
    rows = top.shape[0]
    top[...] = before[:rows, :]
    bottom[...] = behind[rows:, :]


def advance(t0, t1, t2, t3, state, chosen, code_rows):
    total = (
        t0[...].astype(F32) + t1[...].astype(F32) + t2[...].astype(F32) + t3[...].astype(F32)
    )
    middle = (state[...].astype(F32) + total).astype(BF)
    return (dot(chosen[...], middle) + code_rows[...].astype(F32)).astype(BF)


def owner_kernel(t0, t1, t2, t3, state, chosen, code_rows, gain, out_state, out_normed):
    now = advance(t0, t1, t2, t3, state, chosen, code_rows)
    out_state[...] = now
    out_normed[...] = normalize(now.astype(F32), gain[...]).astype(BF)


def owner_last_kernel(
    t0, t1, t2, t3, state, chosen, code_rows, gain, pool, mean_code, out_base, out_normed
):
    now = advance(t0, t1, t2, t3, state, chosen, code_rows)
    out_normed[...] = normalize(now.astype(F32), gain[...]).astype(BF)
    rows = state.shape[0]
    out_base[...] = dot(pool[:, :rows], now) + mean_code[...]


def prepare_kernel(
    code, parent, table,
    rows0, rows1, rows2, mean_code, pool, chosen1, chosen2, code_s, parent_s, table_s, sems,
):
    pairs = ((code, code_s), (parent, parent_s), (table, table_s))
    copies = [pltpu.make_async_copy(a, b, sems.at[k]) for k, (a, b) in enumerate(pairs)]
    for copy in copies:
        copy.start()
    codes = table.shape[0]
    requests, _, beams = code.shape
    spots = requests * beams
    own = rows1.shape[0]
    base = lax.axis_index("mp") * (own // beams)
    row = lax.broadcasted_iota(jnp.int32, (spots, beams), 0)
    lane = lax.broadcasted_iota(jnp.int32, (spots, beams), 1)
    spread = (lane == (row // beams + base) % requests).astype(BF)
    kept = lane == row % beams

    def column(values):
        wide = dot(spread, values.astype(F32).astype(BF))
        return jnp.sum(jnp.where(kept, wide, 0.0), axis=1, keepdims=True).astype(jnp.int32)

    def picked(ids):
        names = lax.broadcasted_iota(jnp.int32, (ids.shape[0], codes), 1)
        return dot((ids == names).astype(BF), table_s[...]).astype(BF)

    copies[0].wait()
    columns = [column(code_s[:, k, :]) for k in range(3)]
    copies[1].wait()
    block = lax.broadcasted_iota(jnp.int32, (own, 1), 0) // beams * beams
    places = lax.broadcasted_iota(jnp.int32, (own, own), 1)
    for k, out in ((1, chosen1), (2, chosen2)):
        out[...] = (column(parent_s[:, k, :])[:own] + block == places).astype(BF)
    code3 = code_s[:, 3, :]
    parent3 = parent_s[:, 3, :]
    tally = jnp.zeros((requests, codes), F32)
    names = lax.broadcasted_iota(jnp.int32, (requests, codes), 1)
    kids = jnp.zeros((requests, spots), F32)
    lanes = lax.broadcasted_iota(jnp.int32, (requests, spots), 1)
    for b in range(beams):
        tally = tally + (code3[:, b : b + 1] == names).astype(F32)
        kids = kids + (parent3[:, b : b + 1] == lanes % beams).astype(F32)
    held = (base + lanes // beams) % requests
    mine = held == lax.broadcasted_iota(jnp.int32, (requests, spots), 0)
    pool[...] = jnp.where(mine, kids / beams, 0.0).astype(BF)
    number = lax.broadcasted_iota(jnp.int32, (requests, codes), 0)
    ours = (number >= base) & (number < base + own // beams)
    copies[2].wait()
    rows0[...] = picked(columns[0])
    rows1[...] = picked(columns[1][:own])
    rows2[...] = picked(columns[2][:own])
    mean_code[...] = dot(jnp.where(ours, tally / beams, 0.0).astype(BF), table_s[...])


def pool_kernel(t0, t1, t2, t3, out):
    out[...] = (
        t0[...].astype(F32) + t1[...].astype(F32) + t2[...].astype(F32) + t3[...].astype(F32)
    ).astype(BF)


def name_places(owners, local_rows, outgoing, target):
    requests, slots = local_rows.shape
    count, capacity = outgoing.shape
    before = (
        lax.broadcasted_iota(jnp.int32, (slots, slots), 0)
        < lax.broadcasted_iota(jnp.int32, (slots, slots), 1)
    ).astype(BF)
    names = lax.broadcasted_iota(jnp.int32, (count, slots), 0)
    places = lax.broadcasted_iota(jnp.int32, (128, slots), 0)
    carry = jnp.zeros((count, 1), F32)
    low = jnp.zeros((count, 128), F32)
    high = jnp.zeros((count, 128), F32)
    lines = []
    for q in range(requests):
        owner = owners[q]
        row = local_rows[q : q + 1, :]
        named = (owner == names).astype(F32)
        ahead = dot(named.astype(BF), before) + carry
        carry = carry + jnp.sum(named, axis=1, keepdims=True)
        position = jnp.sum(named * ahead, axis=0, keepdims=True).astype(jnp.int32)
        lines.append(owner * capacity + position)
        spot = (places == position).astype(BF)
        low = low + lax.dot_general(
            (named * (row & 31).astype(F32)).astype(BF), spot, NT, preferred_element_type=F32
        )
        high = high + lax.dot_general(
            (named * (row >> 5).astype(F32)).astype(BF), spot, NT, preferred_element_type=F32
        )
    outgoing[...] = (high * 32.0 + low).astype(jnp.int32)[:, :capacity]
    spare = jnp.zeros((target.shape[0] - requests, slots), jnp.int32)
    target[...] = jnp.concatenate(lines + [spare], axis=0)


def table_kernel(features, proj, table):
    table[...] = dot(features[...], proj[...]).astype(BF)


def serve_kernel(wanted, table, out, *, group):
    rows = table.shape[0]
    count, capacity, _ = out.shape
    asked = jnp.transpose(wanted[...])
    ids = lax.broadcasted_iota(jnp.int32, (capacity * group, rows), 1)
    for g in range(0, count, group):
        column = jnp.concatenate([asked[:, g + k : g + k + 1] for k in range(group)], axis=0)
        found = dot((column == ids).astype(BF), table[...]).astype(BF)
        for k in range(group):
            out[g + k] = found[k * capacity : (k + 1) * capacity, :]


def rank_kernel(target, returned, bias, out, *, first):
    requests = out.shape[0]
    count, capacity, width = returned.shape
    table = returned[...].reshape(count * capacity, width)
    targets = jnp.transpose(target[...])
    slots = targets.shape[0]
    ids = lax.broadcasted_iota(jnp.int32, (slots, count * capacity), 1)
    for q in range(requests):
        mine = targets[:, first + q : first + q + 1]
        rows = dot((mine == ids).astype(BF), table).astype(BF)
        queries = rows[:CMAX, :ATT]
        keys = rows[CMAX:, :ATT]
        scores = lax.dot_general(queries, keys, NT, preferred_element_type=F32) / math.sqrt(ATT)
        weights = jax.nn.sigmoid(scores).astype(BF)
        interest = dot(weights, rows[CMAX:, ATT:]) / math.sqrt(HIST)
        out[q] = jnp.transpose(interest + rows[:CMAX, ATT:].astype(F32) + bias[...])


def logit_kernel(counts, users, user_proj, units0, units1, weight, out):
    half, values, _ = units0.shape
    requests = out.shape[0]
    terms = jnp.transpose(dot(users[...], user_proj[...]))
    base = lax.axis_index("mp") * requests
    rows = lax.broadcasted_iota(jnp.int32, terms.shape, 1)
    lanes = lax.broadcasted_iota(jnp.int32, (1, CMAX), 1)
    scale = jnp.transpose(jnp.broadcast_to(weight[...], (8, values)))[:, :1]
    for q in range(requests):
        term = jnp.sum(jnp.where(rows == base + q, terms, 0.0), axis=1, keepdims=True)
        unit = units0[q] if q < half else units1[q - half]
        hidden = jnp.maximum(unit + term, 0.0) * scale
        line = jnp.sum(hidden, axis=0, keepdims=True)
        out[q : q + 1, :] = jnp.where(lanes < counts[q], line, 0.0)


def body(
    prompt_state,
    beam_parent,
    beam_code,
    norm_gain,
    up_weight,
    down_weight,
    code_table,
    item_features,
    lookup_owner,
    lookup_row,
    cand_count,
    item_proj,
    user_proj,
    rank_bias,
    out_weight,
):
    requests, width = prompt_state.shape
    beams = beam_parent.shape[2]
    hidden = up_weight.shape[1]
    rows = requests * beams
    rank_rows, slots = lookup_row.shape
    own = rank_rows * beams
    owner_count = lax.axis_size("dp")
    capacity = max(2, 2 * rank_rows * slots // owner_count)
    columns = item_proj.shape[1]
    gain = norm_gain.reshape(1, width)
    shape = jax.ShapeDtypeStruct
    DMA = pltpu.SemaphoreType.DMA

    outgoing, target, part, prompt, gain, up, down = call(
        start_kernel, "start",
        (
            shape((owner_count, capacity), jnp.int32), shape((8, slots), jnp.int32),
            shape((requests, width), BF), shape((requests, width), BF), shape((1, width), F32),
            shape((width, hidden), BF), shape((hidden, width), BF),
        ),
        [HBM] * 6, (VMEM,) * 7,
        (
            pltpu.VMEM((rank_rows, 1, slots), jnp.int32), pltpu.VMEM((rank_rows, slots), jnp.int32),
            pltpu.VMEM((requests, hidden), BF), DMA((6,)),
        ),
        limit=40, flops=100 * rows * width * hidden, moved=1_000_000,
    )(
        jnp.transpose(lookup_owner, (0, 2, 1)), lookup_row, prompt_state, gain,
        up_weight, down_weight,
    )
    parts = [shift(part, "mp", k) for k in (1, 2, 3)]
    began = part
    rows0, rows1, rows2, mean_code, pool, chosen1, chosen2 = call(
        prepare_kernel, "prepare",
        (
            shape((rows, width), BF), shape((own, width), BF), shape((own, width), BF),
            shape((requests, width), F32), shape((requests, rows), BF),
            shape((own, own), BF), shape((own, own), BF),
        ),
        [HBM] * 3, (VMEM,) * 7,
        (
            pltpu.VMEM(beam_code.shape, jnp.int32), pltpu.VMEM(beam_parent.shape, jnp.int32),
            pltpu.VMEM(code_table.shape, BF), DMA((3,)),
        ),
        limit=16, flops=2 * 400 * 256 * width, moved=3_000_000,
    )(beam_code, after(beam_parent, part), code_table)
    ffn = dict(limit=16, flops=4 * rows * width * hidden, moved=50 * width * hidden)

    def shared(normed, ringed):
        if not ringed:
            return [normed] + [shift(normed, "mp", -k) for k in (1, 2, 3)]
        behind, before = shift(normed, "mp", -1), shift(normed, "mp", 1)
        top, bottom = call(
            halves_kernel, "halves", (shape((own // 2, width), BF),) * 2, [VMEM] * 2, (VMEM,) * 2,
            limit=16, flops=1000, moved=1_000_000,
        )(before, behind)
        return [normed, behind, shift(top, "mp", 1), shift(bottom, "mp", -1), before]

    quarter = (shape((own, width), BF),) * 4
    *outs, state = call(
        second_kernel, "ffn1", quarter + (shape((own, width), BF),),
        [VMEM] * 9, (VMEM,) * 5,
        (pltpu.VMEM((rows, hidden), BF),
         pltpu.VMEM((2 * requests, width), F32), pltpu.VMEM((rows, width), BF)),
        **ffn,
    )(prompt, part, *parts, rows0, gain, up, down)
    outgoing = after(outgoing, outs[0])
    wanted = lax.all_to_all(outgoing, "dp", split_axis=0, concat_axis=0, tiled=True)
    sums = [outs[0]] + [shift(outs[k], "mp", k) for k in (1, 2, 3)]
    state, normed = call(
        owner_kernel, "owner1", (shape((own, width), BF),) * 2, [VMEM] * 8, (VMEM,) * 2,
        limit=16, flops=2 * own * own * width, moved=2_000_000,
    )(*sums, state, chosen1, rows1, gain)

    up, down = call(
        load_kernel, "load", (shape((width, hidden), BF), shape((hidden, width), BF)),
        [HBM] * 2, (VMEM,) * 2, (DMA((2,)),), limit=40, flops=20 * rows * width * hidden, moved=1_000_000,
    )(after(up_weight, normed), after(down_weight, normed))
    wanted = after(wanted, normed)
    others = shared(normed, False)
    outs = call(
        third_kernel, "ffn2", quarter, [VMEM] * (len(others) + 2), (VMEM,) * 4,
        (pltpu.VMEM((rows, hidden), BF), pltpu.VMEM((rows, width), BF)),
        **ffn,
    )(*others, up, down)
    sums = [outs[0]] + [shift(outs[k], "mp", k) for k in (1, 2, 3)]
    base, normed = call(
        owner_last_kernel, "owner2", (shape((requests, width), F32), shape((own, width), BF)),
        [VMEM] * 10, (VMEM,) * 2,
        limit=16, flops=2 * own * own * width, moved=2_000_000,
    )(*sums, state, chosen2, rows2, gain, pool, mean_code)

    others = shared(normed, False)
    part = call(
        last_kernel, "ffn3", shape((requests, width), BF), [VMEM] * (len(others) + 4), VMEM,
        (pltpu.VMEM((rows, hidden), BF), pltpu.VMEM((rows, width), BF)),
        **ffn,
    )(*others, pool, base, up, down)
    parts = [shift(part, "mp", k) for k in (1, 2, 3)]
    table = call(
        table_kernel, "table", shape((item_features.shape[0], columns), BF), [VMEM] * 2, VMEM,
        limit=16, flops=2 * item_features.size * columns, moved=4_000_000,
    )(item_features, after(item_proj, began))
    served = call(
        functools.partial(serve_kernel, group=4), "serve",
        shape((owner_count, capacity, columns), BF), [VMEM] * 2, VMEM, limit=16,
        flops=2 * owner_count * capacity * item_features.shape[0] * columns, moved=4_000_000,
    )(wanted, table)
    returned = lax.all_to_all(served, "dp", split_axis=0, concat_axis=0, tiled=True)
    returned = after(returned, part)
    def ranked(first, count, blocks):
        return call(
            functools.partial(rank_kernel, first=first), f"rank{first}",
            shape((count, columns - ATT, CMAX), F32), [VMEM] * 3, VMEM, limit=16,
            flops=2 * count * slots * owner_count * capacity * columns, moved=4_000_000,
        )(target, blocks, rank_bias.reshape(1, -1))

    early = rank_rows // 2
    units = [ranked(0, early, returned)]
    pooled = call(
        pool_kernel, "pool", shape((requests, width), BF), [VMEM] * 4, VMEM,
        limit=16, flops=100_000, moved=400_000,
    )(after(part, units[0]), *parts)
    partner = swapped(pooled, "section", 0)
    units.append(ranked(early, rank_rows - early, after(returned, pooled)))

    logits = call(
        logit_kernel, "logit", shape((rank_rows, CMAX), F32), [SMEM] + [VMEM] * 5, VMEM,
        limit=16, flops=20_000_000, moved=1_600_000,
    )(cand_count, partner, user_proj, *units, out_weight.reshape(1, -1))
    return (logits, pooled)


def solution(mesh):
    in_specs = (
        P(("section", "dp"), None),
        P(("section", "dp"), None, None),
        P(("section", "dp"), None, None),
        P(),
        P(None, "mp"),
        P("mp", None),
        P(),
        P("dp", None),
        P(("section", "dp", "mp"), None, None),
        P(("section", "dp", "mp"), None),
        P(("section", "dp", "mp")),
        P(),
        P(),
        P(),
        P(),
    )
    out_specs = (P(("section", "dp", "mp"), None), P(("section", "dp"), None))
    return jax.shard_map(body, mesh=mesh, in_specs=in_specs, out_specs=out_specs, check_vma=False)
```

```python
import functools
import math

import jax
import jax.numpy as jnp
from jax import lax
from jax.experimental import pallas as pl
from jax.experimental.pallas import tpu as pltpu
from jax.sharding import PartitionSpec as P

ATT = 128
CMAX = 128
HIST = 256
UP_CUTS = 4
DOWN_CUTS = 4
BF = jnp.bfloat16
F32 = jnp.float32
NT = (((1,), (1,)), ((), ()))

VMEM = pl.BlockSpec(memory_space=pltpu.VMEM)
SMEM = pl.BlockSpec(memory_space=pltpu.SMEM)
HBM = pl.BlockSpec(memory_space=pltpu.HBM)


def dot(a, b):
    return jnp.dot(a, b, preferred_element_type=F32)


def call(kernel, name, out_shape, in_specs, out_specs, scratch=(), limit=16, flops=0, moved=0):
    return pl.pallas_call(
        kernel,
        name=name,
        out_shape=out_shape,
        in_specs=in_specs,
        out_specs=out_specs,
        scratch_shapes=list(scratch),
        compiler_params=pltpu.CompilerParams(vmem_limit_bytes=limit * 2**20),
        cost_estimate=pl.CostEstimate(flops=flops, bytes_accessed=moved, transcendentals=0),
    )


def shift(value, axis, by):
    size = lax.axis_size(axis)
    return lax.ppermute(value, axis, [(i, (i + by) % size) for i in range(size)])


def swapped(value, axis, bit):
    mask = 2**bit
    pairs = [(source, source ^ mask) for source in range(lax.axis_size(axis))]
    return lax.ppermute(value, axis, pairs)


def after(value, earlier):
    return lax.optimization_barrier((value, earlier))[0]


def normalize(values, gain_row):
    squares = jnp.mean(values * values, axis=-1, keepdims=True)
    return values * lax.rsqrt(squares + 1e-06) * gain_row


def raise_rows(normed, up, act_s):
    wide = up.shape[1] // UP_CUTS
    for c in range(UP_CUTS):
        cut = slice(c * wide, (c + 1) * wide)
        act_s[:, cut] = jax.nn.gelu(dot(normed, up[:, cut])).astype(BF)


def start_kernel(
    owners, local_rows, prompt, gain, up, down,
    outgoing, target, part, prompt_v, gain_v, up_v, down_v, owners_s, local_s, act_s, sems,
):
    pairs = (
        (owners, owners_s), (local_rows, local_s), (prompt, prompt_v), (gain, gain_v),
        (up, up_v), (down, down_v),
    )
    copies = [pltpu.make_async_copy(a, b, sems.at[k]) for k, (a, b) in enumerate(pairs)]
    for copy in copies:
        copy.start()
    copies[0].wait()
    copies[1].wait()
    name_places(owners_s, local_s, outgoing, target)
    copies[2].wait()
    copies[3].wait()
    normed = normalize(prompt_v[...].astype(F32), gain_v[...]).astype(BF)
    copies[4].wait()
    raise_rows(normed, up_v, act_s)
    copies[5].wait()
    part[...] = dot(act_s[...], down_v[...]).astype(BF)


def load_kernel(up, down, up_v, down_v, sems):
    copies = [
        pltpu.make_async_copy(up, up_v, sems.at[0]),
        pltpu.make_async_copy(down, down_v, sems.at[1]),
    ]
    for copy in copies:
        copy.start()
    for copy in copies:
        copy.wait()


def lower(act_s, down, outs):
    tall = down.shape[1] // DOWN_CUTS
    own = outs[0].shape[0]
    for c in range(DOWN_CUTS):
        cut = slice(c * tall, (c + 1) * tall)
        part = dot(act_s[...], down[:, cut]).astype(BF)
        for k, out in enumerate(outs):
            out[:, cut] = part[k * own : (k + 1) * own, :]


def second_kernel(
    prompt, t0, t1, t2, t3, code_rows, gain, up, down,
    o0, o1, o2, o3, state, act_s, middle_s, normed_s,
):
    requests = prompt.shape[0]
    beams = code_rows.shape[0] // requests
    own = o0.shape[0]
    total = (
        t0[...].astype(F32) + t1[...].astype(F32) + t2[...].astype(F32) + t3[...].astype(F32)
    )
    middle = (prompt[...].astype(F32) + total).astype(BF).astype(F32)
    middle_s[0:requests, :] = middle
    middle_s[requests : 2 * requests, :] = middle
    base = lax.axis_index("mp") * (own // beams)
    for r in range(requests):
        row = middle_s[pl.ds(base + r, 1), :]
        now = (row + code_rows[r * beams : (r + 1) * beams, :].astype(F32)).astype(BF)
        if (r + 1) * beams <= own:
            state[r * beams : (r + 1) * beams, :] = now
        normed_s[r * beams : (r + 1) * beams, :] = normalize(now.astype(F32), gain[...]).astype(BF)
    raise_rows(normed_s[...], up, act_s)
    lower(act_s, down, (o0, o1, o2, o3))


def gathered(blocks, normed_s):
    first = 0
    for ref in blocks:
        normed_s[first : first + ref.shape[0], :] = ref[...]
        first += ref.shape[0]
    return normed_s[...]


def third_kernel(*refs):
    *blocks, up, down, o0, o1, o2, o3, act_s, normed_s = refs
    raise_rows(gathered(blocks, normed_s), up, act_s)
    lower(act_s, down, (o0, o1, o2, o3))


def last_kernel(*refs):
    *blocks, pool, base, up, down, out, act_s, normed_s = refs
    raise_rows(gathered(blocks, normed_s), up, act_s)
    mixed = dot(pool[...], act_s[...]).astype(BF)
    out[...] = (dot(mixed, down[...]) + base[...]).astype(BF)


def halves_kernel(before, behind, top, bottom):
    rows = top.shape[0]
    top[...] = before[:rows, :]
    bottom[...] = behind[rows:, :]


def advance(t0, t1, t2, t3, state, chosen, code_rows):
    total = (
        t0[...].astype(F32) + t1[...].astype(F32) + t2[...].astype(F32) + t3[...].astype(F32)
    )
    middle = (state[...].astype(F32) + total).astype(BF)
    return (dot(chosen[...], middle) + code_rows[...].astype(F32)).astype(BF)


def owner_kernel(t0, t1, t2, t3, state, chosen, code_rows, gain, out_state, out_normed):
    now = advance(t0, t1, t2, t3, state, chosen, code_rows)
    out_state[...] = now
    out_normed[...] = normalize(now.astype(F32), gain[...]).astype(BF)


def owner_last_kernel(
    t0, t1, t2, t3, state, chosen, code_rows, gain, pool, mean_code, out_base, out_normed
):
    now = advance(t0, t1, t2, t3, state, chosen, code_rows)
    out_normed[...] = normalize(now.astype(F32), gain[...]).astype(BF)
    rows = state.shape[0]
    out_base[...] = dot(pool[:, :rows], now) + mean_code[...]


def prepare_kernel(
    code, parent, table,
    rows0, rows1, rows2, mean_code, pool, chosen1, chosen2, code_s, parent_s, table_s, sems,
):
    pairs = ((code, code_s), (parent, parent_s), (table, table_s))
    copies = [pltpu.make_async_copy(a, b, sems.at[k]) for k, (a, b) in enumerate(pairs)]
    for copy in copies:
        copy.start()
    codes = table.shape[0]
    requests, _, beams = code.shape
    spots = requests * beams
    own = rows1.shape[0]
    base = lax.axis_index("mp") * (own // beams)
    row = lax.broadcasted_iota(jnp.int32, (spots, beams), 0)
    lane = lax.broadcasted_iota(jnp.int32, (spots, beams), 1)
    spread = (lane == (row // beams + base) % requests).astype(BF)
    kept = lane == row % beams

    def column(values):
        wide = dot(spread, values.astype(F32).astype(BF))
        return jnp.sum(jnp.where(kept, wide, 0.0), axis=1, keepdims=True).astype(jnp.int32)

    def picked(ids):
        names = lax.broadcasted_iota(jnp.int32, (ids.shape[0], codes), 1)
        return dot((ids == names).astype(BF), table_s[...]).astype(BF)

    copies[0].wait()
    columns = [column(code_s[:, k, :]) for k in range(3)]
    copies[1].wait()
    block = lax.broadcasted_iota(jnp.int32, (own, 1), 0) // beams * beams
    places = lax.broadcasted_iota(jnp.int32, (own, own), 1)
    for k, out in ((1, chosen1), (2, chosen2)):
        out[...] = (column(parent_s[:, k, :])[:own] + block == places).astype(BF)
    code3 = code_s[:, 3, :]
    parent3 = parent_s[:, 3, :]
    tally = jnp.zeros((requests, codes), F32)
    names = lax.broadcasted_iota(jnp.int32, (requests, codes), 1)
    kids = jnp.zeros((requests, spots), F32)
    lanes = lax.broadcasted_iota(jnp.int32, (requests, spots), 1)
    for b in range(beams):
        tally = tally + (code3[:, b : b + 1] == names).astype(F32)
        kids = kids + (parent3[:, b : b + 1] == lanes % beams).astype(F32)
    held = (base + lanes // beams) % requests
    mine = held == lax.broadcasted_iota(jnp.int32, (requests, spots), 0)
    pool[...] = jnp.where(mine, kids / beams, 0.0).astype(BF)
    number = lax.broadcasted_iota(jnp.int32, (requests, codes), 0)
    ours = (number >= base) & (number < base + own // beams)
    copies[2].wait()
    rows0[...] = picked(columns[0])
    rows1[...] = picked(columns[1][:own])
    rows2[...] = picked(columns[2][:own])
    mean_code[...] = dot(jnp.where(ours, tally / beams, 0.0).astype(BF), table_s[...])


def pool_kernel(t0, t1, t2, t3, out):
    out[...] = (
        t0[...].astype(F32) + t1[...].astype(F32) + t2[...].astype(F32) + t3[...].astype(F32)
    ).astype(BF)


def name_places(owners, local_rows, outgoing, target):
    requests, slots = local_rows.shape
    count, capacity = outgoing.shape
    before = (
        lax.broadcasted_iota(jnp.int32, (slots, slots), 0)
        < lax.broadcasted_iota(jnp.int32, (slots, slots), 1)
    ).astype(BF)
    names = lax.broadcasted_iota(jnp.int32, (count, slots), 0)
    places = lax.broadcasted_iota(jnp.int32, (128, slots), 0)
    carry = jnp.zeros((count, 1), F32)
    low = jnp.zeros((count, 128), F32)
    high = jnp.zeros((count, 128), F32)
    lines = []
    for q in range(requests):
        owner = owners[q]
        row = local_rows[q : q + 1, :]
        named = (owner == names).astype(F32)
        ahead = dot(named.astype(BF), before) + carry
        carry = carry + jnp.sum(named, axis=1, keepdims=True)
        position = jnp.sum(named * ahead, axis=0, keepdims=True).astype(jnp.int32)
        lines.append(owner * capacity + position)
        spot = (places == position).astype(BF)
        low = low + lax.dot_general(
            (named * (row & 31).astype(F32)).astype(BF), spot, NT, preferred_element_type=F32
        )
        high = high + lax.dot_general(
            (named * (row >> 5).astype(F32)).astype(BF), spot, NT, preferred_element_type=F32
        )
    outgoing[...] = (high * 32.0 + low).astype(jnp.int32)[:, :capacity]
    spare = jnp.zeros((target.shape[0] - requests, slots), jnp.int32)
    target[...] = jnp.concatenate(lines + [spare], axis=0)


def table_kernel(features, proj, table):
    table[...] = dot(features[...], proj[...]).astype(BF)


def serve_kernel(wanted, table, out, found_s, sems, *, group):
    rows = table.shape[0]
    count, capacity, _ = out.shape
    asked = jnp.transpose(wanted[...])
    ids = lax.broadcasted_iota(jnp.int32, (capacity * group, rows), 1)
    sends = []
    for g in range(0, count, group):
        column = jnp.concatenate([asked[:, g + k : g + k + 1] for k in range(group)], axis=0)
        found = dot((column == ids).astype(BF), table[...]).astype(BF)
        for k in range(group):
            found_s[g + k] = found[k * capacity : (k + 1) * capacity, :]
        cut = pl.ds(g, group)
        sends.append(pltpu.make_async_copy(found_s.at[cut], out.at[cut], sems.at[g // group]))
        sends[-1].start()
    for send in sends:
        send.wait()


def rank_kernel(target, returned, bias, out, *, first):
    requests = out.shape[0]
    count, capacity, width = returned.shape
    table = returned[...].reshape(count * capacity, width)
    targets = jnp.transpose(target[...])
    slots = targets.shape[0]
    ids = lax.broadcasted_iota(jnp.int32, (slots, count * capacity), 1)
    for q in range(requests):
        mine = targets[:, first + q : first + q + 1]
        rows = dot((mine == ids).astype(BF), table).astype(BF)
        queries = rows[:CMAX, :ATT]
        keys = rows[CMAX:, :ATT]
        scores = lax.dot_general(queries, keys, NT, preferred_element_type=F32) / math.sqrt(ATT)
        weights = jax.nn.sigmoid(scores).astype(BF)
        interest = dot(weights, rows[CMAX:, ATT:]) / math.sqrt(HIST)
        out[q] = jnp.transpose(interest + rows[:CMAX, ATT:].astype(F32) + bias[...])


def logit_kernel(counts, users, user_proj, units0, units1, weight, out):
    half, values, _ = units0.shape
    requests = out.shape[0]
    terms = jnp.transpose(dot(users[...], user_proj[...]))
    base = lax.axis_index("mp") * requests
    rows = lax.broadcasted_iota(jnp.int32, terms.shape, 1)
    lanes = lax.broadcasted_iota(jnp.int32, (1, CMAX), 1)
    scale = jnp.transpose(jnp.broadcast_to(weight[...], (8, values)))[:, :1]
    for q in range(requests):
        term = jnp.sum(jnp.where(rows == base + q, terms, 0.0), axis=1, keepdims=True)
        unit = units0[q] if q < half else units1[q - half]
        hidden = jnp.maximum(unit + term, 0.0) * scale
        line = jnp.sum(hidden, axis=0, keepdims=True)
        out[q : q + 1, :] = jnp.where(lanes < counts[q], line, 0.0)


def body(
    prompt_state,
    beam_parent,
    beam_code,
    norm_gain,
    up_weight,
    down_weight,
    code_table,
    item_features,
    lookup_owner,
    lookup_row,
    cand_count,
    item_proj,
    user_proj,
    rank_bias,
    out_weight,
):
    requests, width = prompt_state.shape
    beams = beam_parent.shape[2]
    hidden = up_weight.shape[1]
    rows = requests * beams
    rank_rows, slots = lookup_row.shape
    own = rank_rows * beams
    owner_count = lax.axis_size("dp")
    capacity = max(2, 2 * rank_rows * slots // owner_count)
    columns = item_proj.shape[1]
    gain = norm_gain.reshape(1, width)
    shape = jax.ShapeDtypeStruct
    DMA = pltpu.SemaphoreType.DMA

    outgoing, target, part, prompt, gain, up, down = call(
        start_kernel, "start",
        (
            shape((owner_count, capacity), jnp.int32), shape((8, slots), jnp.int32),
            shape((requests, width), BF), shape((requests, width), BF), shape((1, width), F32),
            shape((width, hidden), BF), shape((hidden, width), BF),
        ),
        [HBM] * 6, (VMEM,) * 7,
        (
            pltpu.VMEM((rank_rows, 1, slots), jnp.int32), pltpu.VMEM((rank_rows, slots), jnp.int32),
            pltpu.VMEM((requests, hidden), BF), DMA((6,)),
        ),
        limit=40, flops=100 * rows * width * hidden, moved=1_000_000,
    )(
        jnp.transpose(lookup_owner, (0, 2, 1)), lookup_row, prompt_state, gain,
        up_weight, down_weight,
    )
    parts = [shift(part, "mp", k) for k in (1, 2, 3)]
    began = part
    rows0, rows1, rows2, mean_code, pool, chosen1, chosen2 = call(
        prepare_kernel, "prepare",
        (
            shape((rows, width), BF), shape((own, width), BF), shape((own, width), BF),
            shape((requests, width), F32), shape((requests, rows), BF),
            shape((own, own), BF), shape((own, own), BF),
        ),
        [HBM] * 3, (VMEM,) * 7,
        (
            pltpu.VMEM(beam_code.shape, jnp.int32), pltpu.VMEM(beam_parent.shape, jnp.int32),
            pltpu.VMEM(code_table.shape, BF), DMA((3,)),
        ),
        limit=16, flops=2 * 400 * 256 * width, moved=3_000_000,
    )(beam_code, after(beam_parent, part), code_table)
    ffn = dict(limit=16, flops=4 * rows * width * hidden, moved=50 * width * hidden)

    def shared(normed, ringed):
        if not ringed:
            return [normed] + [shift(normed, "mp", -k) for k in (1, 2, 3)]
        behind, before = shift(normed, "mp", -1), shift(normed, "mp", 1)
        top, bottom = call(
            halves_kernel, "halves", (shape((own // 2, width), BF),) * 2, [VMEM] * 2, (VMEM,) * 2,
            limit=16, flops=1000, moved=1_000_000,
        )(before, behind)
        return [normed, behind, shift(top, "mp", 1), shift(bottom, "mp", -1), before]

    quarter = (shape((own, width), BF),) * 4
    *outs, state = call(
        second_kernel, "ffn1", quarter + (shape((own, width), BF),),
        [VMEM] * 9, (VMEM,) * 5,
        (pltpu.VMEM((rows, hidden), BF),
         pltpu.VMEM((2 * requests, width), F32), pltpu.VMEM((rows, width), BF)),
        **ffn,
    )(prompt, part, *parts, rows0, gain, up, down)
    outgoing = after(outgoing, outs[0])
    wanted = lax.all_to_all(outgoing, "dp", split_axis=0, concat_axis=0, tiled=True)
    sums = [outs[0]] + [shift(outs[k], "mp", k) for k in (1, 2, 3)]
    state, normed = call(
        owner_kernel, "owner1", (shape((own, width), BF),) * 2, [VMEM] * 8, (VMEM,) * 2,
        limit=16, flops=2 * own * own * width, moved=2_000_000,
    )(*sums, state, chosen1, rows1, gain)

    up, down = call(
        load_kernel, "load", (shape((width, hidden), BF), shape((hidden, width), BF)),
        [HBM] * 2, (VMEM,) * 2, (DMA((2,)),), limit=40, flops=20 * rows * width * hidden, moved=1_000_000,
    )(after(up_weight, normed), after(down_weight, normed))
    wanted = after(wanted, normed)
    others = shared(normed, False)
    outs = call(
        third_kernel, "ffn2", quarter, [VMEM] * (len(others) + 2), (VMEM,) * 4,
        (pltpu.VMEM((rows, hidden), BF), pltpu.VMEM((rows, width), BF)),
        **ffn,
    )(*others, up, down)
    sums = [outs[0]] + [shift(outs[k], "mp", k) for k in (1, 2, 3)]
    base, normed = call(
        owner_last_kernel, "owner2", (shape((requests, width), F32), shape((own, width), BF)),
        [VMEM] * 10, (VMEM,) * 2,
        limit=16, flops=2 * own * own * width, moved=2_000_000,
    )(*sums, state, chosen2, rows2, gain, pool, mean_code)

    others = shared(normed, False)
    part = call(
        last_kernel, "ffn3", shape((requests, width), BF), [VMEM] * (len(others) + 4), VMEM,
        (pltpu.VMEM((rows, hidden), BF), pltpu.VMEM((rows, width), BF)),
        **ffn,
    )(*others, pool, base, up, down)
    parts = [shift(part, "mp", k) for k in (1, 2, 3)]
    table = call(
        table_kernel, "table", shape((item_features.shape[0], columns), BF), [VMEM] * 2, VMEM,
        limit=16, flops=2 * item_features.size * columns, moved=4_000_000,
    )(item_features, after(item_proj, began))
    served = call(
        functools.partial(serve_kernel, group=4), "serve",
        shape((owner_count, capacity, columns), BF), [VMEM] * 2, HBM,
        (pltpu.VMEM((owner_count, capacity, columns), BF), DMA((owner_count // 4,))), limit=58,
        flops=2 * owner_count * capacity * item_features.shape[0] * columns, moved=4_000_000,
    )(wanted, table)
    returned = lax.all_to_all(served, "dp", split_axis=0, concat_axis=0, tiled=True)
    returned = after(returned, part)
    def ranked(first, count, blocks):
        return call(
            functools.partial(rank_kernel, first=first), f"rank{first}",
            shape((count, columns - ATT, CMAX), F32), [VMEM] * 3, VMEM, limit=16,
            flops=2 * count * slots * owner_count * capacity * columns, moved=4_000_000,
        )(target, blocks, rank_bias.reshape(1, -1))

    early = rank_rows // 2
    units = [ranked(0, early, returned)]
    pooled = call(
        pool_kernel, "pool", shape((requests, width), BF), [VMEM] * 4, VMEM,
        limit=16, flops=100_000, moved=400_000,
    )(after(part, units[0]), *parts)
    partner = swapped(pooled, "section", 0)
    units.append(ranked(early, rank_rows - early, after(returned, pooled)))

    logits = call(
        logit_kernel, "logit", shape((rank_rows, CMAX), F32), [SMEM] + [VMEM] * 5, VMEM,
        limit=16, flops=20_000_000, moved=1_600_000,
    )(cand_count, partner, user_proj, *units, out_weight.reshape(1, -1))
    return (logits, pooled)


def solution(mesh):
    in_specs = (
        P(("section", "dp"), None),
        P(("section", "dp"), None, None),
        P(("section", "dp"), None, None),
        P(),
        P(None, "mp"),
        P("mp", None),
        P(),
        P("dp", None),
        P(("section", "dp", "mp"), None, None),
        P(("section", "dp", "mp"), None),
        P(("section", "dp", "mp")),
        P(),
        P(),
        P(),
        P(),
    )
    out_specs = (P(("section", "dp", "mp"), None), P(("section", "dp"), None))
    return jax.shard_map(body, mesh=mesh, in_specs=in_specs, out_specs=out_specs, check_vma=False)
```
